128 devices in a mesh: dp: 8 (over x_lo, z), ctx: 16 (over y, x_hi, core).
Axes of the slice: x: 4 (x_hi: 2, x_lo: 2; x = x_hi * 2 + x_lo), y: 4, z: 4, core: 2. Of those that a mesh axis runs over, the one named last changes fastest.
Arguments:
- queries: bfloat16 [8, 2048, 2048], P('dp', 'ctx'), may hold values from -6 to 6
- key_proj: bfloat16 [8, 2048, 2048], P('dp', 'ctx'), may hold values from -6 to 6
- value_proj: bfloat16 [8, 2048, 2048], P('dp', 'ctx'), may hold values from -6 to 6
- filters: float32 [2048, 2048], P(None, 'ctx'), may hold values from -1.2 to 1.2
- out_weight: bfloat16 [2048, 2048], P('ctx'), may hold values from -0.125 to 0.125
- out_grad: bfloat16 [8, 2048, 2048], P('dp', 'ctx'), may hold values from -6 to 6
Outputs:
- block_out: bfloat16 [8, 2048, 2048], P('dp', 'ctx')
- query_grad: bfloat16 [8, 2048, 2048], P('dp', 'ctx')
- key_grad: bfloat16 [8, 2048, 2048], P('dp', 'ctx')
- value_grad: bfloat16 [8, 2048, 2048], P('dp', 'ctx')
- filter_grad: float32 [2048, 2048], P(None, 'ctx')
- weight_grad: float32 [2048, 2048], P('ctx')
The draws below stay inside these ranges and needn't reach their ends.
All inputs are finite; a program needn't handle non-finite values.
Results may differ from the reference program's by a relative error of at most 0.023.
Values may be sent and summed in bfloat16 or wider, within the bound.
A program may use at most 128 MiB of HBM per device.

```python
import math
import jax
import jax.numpy as jnp
from jax import lax

D = 2048
FILTER_LANES = 2048
CONTEXT_SPAN = 2048
SEQS = 8


def draw_filters(key, part):
    key = jax.random.fold_in(key, 7)
    rate_key, rough_key, location_random_key, drop_random_key = jax.random.split(key, 4)
    letter_indices = jnp.arange(CONTEXT_SPAN, dtype=jnp.float32)[:, None]
    fading_speed = jnp.exp(jax.random.uniform(rate_key, (FILTER_LANES,), jnp.float32, math.log(0.04 / CONTEXT_SPAN), math.log(1.0 / 30.0)))
    noisy_component = jnp.clip(jax.random.normal(rough_key, (CONTEXT_SPAN, FILTER_LANES), jnp.float32), -4.0, 4.0)
    impulse_indices = jax.random.randint(location_random_key, (4,), 0, CONTEXT_SPAN)
    impulse_removals = jax.random.uniform(drop_random_key, (4, FILTER_LANES), jnp.float32, 0.5, 0.8)
    retained_entries = jnp.ones((CONTEXT_SPAN, FILTER_LANES), jnp.float32)
    for letter_index in range(4):
        retained_entries = retained_entries * jnp.where(letter_indices >= impulse_indices[letter_index].astype(jnp.float32), impulse_removals[letter_index][None, :], 1.0)
    return noisy_component * jnp.exp(-fading_speed * letter_indices) * retained_entries * jnp.sqrt(2.0 * fading_speed + 1.0 / CONTEXT_SPAN)


def level_of(key, extent, shards, smallest, high):
    level = 1.0
    for axis_at, parts in shards:
        heights = jax.random.uniform(jax.random.fold_in(jax.random.fold_in(key, 6), axis_at), (parts,), jnp.float32, smallest / len(shards), high / len(shards))
        level = level * jnp.repeat(jnp.exp(heights), extent[axis_at] // parts).reshape((-1,) + (1,) * (len(extent) - 1 - axis_at))
    return level


def centred(stream_key, dims, scale, reach, cuts=(), held_as=jnp.bfloat16):
    entries = jax.random.normal(stream_key, dims, jnp.float32) * scale
    if len(cuts) > 0:
        entries = level_of(stream_key, dims, cuts, -0.22, 0.18) * entries
    return jnp.clip(entries, min=-reach, max=reach).astype(held_as)


def setup_inputs(seed: int = 0) -> dict:
    key_of = jax.random.split(jax.random.key(seed), 7)
    return {
        "queries": centred(key_of[0], (SEQS, CONTEXT_SPAN, FILTER_LANES), 1.0, 6.0, ((0, 8), (1, 16))),
        "key_proj": centred(key_of[1], (SEQS, CONTEXT_SPAN, FILTER_LANES), 1.0, 6.0, ((0, 8), (1, 16))),
        "value_proj": centred(key_of[2], (SEQS, CONTEXT_SPAN, FILTER_LANES), 1.0, 6.0, ((0, 8), (1, 16))),
        "filters": draw_filters(jax.random.fold_in(key_of[6], 71), 0),
        "out_weight": centred(key_of[4], (FILTER_LANES, D), FILTER_LANES ** -0.5, 0.125, ((0, 16),)),
        "out_grad": centred(key_of[5], (SEQS, CONTEXT_SPAN, D), 1.0, 6.0, ((0, 8), (1, 16))),
    }


def reference(queries, key_proj, value_proj, filters, out_weight, out_grad):
    padded_len = 2 * CONTEXT_SPAN
    filter_freq = jnp.fft.rfft(filters, n=padded_len, axis=0)

    def one_sequence(pieces):
        query_rows, key_rows, value_rows, grad_rows = pieces
        mixed = (key_rows.astype(jnp.float32) * value_rows.astype(jnp.float32)).astype(jnp.bfloat16)
        mixed_freq = jnp.fft.rfft(mixed.astype(jnp.float32), n=padded_len, axis=0)
        conv_out = jnp.fft.irfft(mixed_freq * filter_freq, n=padded_len, axis=0)[:CONTEXT_SPAN].astype(jnp.bfloat16)
        gated = (query_rows.astype(jnp.float32) * conv_out.astype(jnp.float32)).astype(jnp.bfloat16)
        block_out = jnp.dot(gated, out_weight, preferred_element_type=jnp.float32).astype(jnp.bfloat16)
        gated_grad = jnp.dot(grad_rows, out_weight.T, preferred_element_type=jnp.float32).astype(jnp.bfloat16)
        query_grad = (gated_grad.astype(jnp.float32) * conv_out.astype(jnp.float32)).astype(jnp.bfloat16)
        conv_grad = (gated_grad.astype(jnp.float32) * query_rows.astype(jnp.float32)).astype(jnp.bfloat16)
        grad_freq = jnp.fft.rfft(conv_grad.astype(jnp.float32), n=padded_len, axis=0)
        mixed_grad = jnp.fft.irfft(jnp.conj(filter_freq) * grad_freq, n=padded_len, axis=0)[:CONTEXT_SPAN].astype(jnp.bfloat16)
        key_grad = (mixed_grad.astype(jnp.float32) * value_rows.astype(jnp.float32)).astype(jnp.bfloat16)
        value_grad = (mixed_grad.astype(jnp.float32) * key_rows.astype(jnp.float32)).astype(jnp.bfloat16)
        filter_term = jnp.fft.irfft(grad_freq * jnp.conj(mixed_freq), n=padded_len, axis=0)[:CONTEXT_SPAN]
        weight_term = jnp.dot(gated.T, grad_rows, preferred_element_type=jnp.float32)
        return (block_out, query_grad, key_grad, value_grad, filter_term, weight_term)
    results = lax.map(one_sequence, (queries, key_proj, value_proj, out_grad))
    norm_scale = 1.0 / math.sqrt(SEQS * CONTEXT_SPAN)
    filter_grad = lax.optimization_barrier(jnp.sum(results[4], axis=0)) * norm_scale
    weight_grad = lax.optimization_barrier(jnp.sum(results[5], axis=0)) * norm_scale
    return (results[0], results[1], results[2], results[3], filter_grad, weight_grad)
```

```python
import math

import jax
import jax.numpy as jnp
import ml_dtypes
import numpy as np
from jax import lax
from jax.experimental import pallas as pl
from jax.experimental.pallas import tpu as pltpu
from jax.sharding import PartitionSpec as P

MESH = pl.DeviceIdType.MESH
BF = jnp.bfloat16
F32 = jnp.float32


def make_tables():
    k0 = np.arange(16)
    t1 = np.arange(16)
    angle = 2.0 * np.pi * (k0[:, None] + 0.5) * t1[None, :] / 32.0
    outer = np.stack([np.cos(angle), -np.sin(angle)], axis=1)
    outer = np.einsum("krt,su->krstu", outer, np.eye(16)).reshape(512, 256)
    t0 = np.arange(128)
    k1 = np.arange(128)
    angle = (k0[:, None, None] + 0.5) * t0[None, None, :] / 4096.0 + (
        (k1[None, :, None] * t0[None, None, :]) % 128
    ) / 128.0
    cos = np.cos(2.0 * np.pi * angle).reshape(16, 128, 8, 16)
    sin = np.sin(2.0 * np.pi * angle).reshape(16, 128, 8, 16)
    inner = np.empty((16, 2, 128, 8, 2, 16))
    inner[:, 0, :, :, 0] = cos
    inner[:, 0, :, :, 1] = sin
    inner[:, 1, :, :, 0] = -sin
    inner[:, 1, :, :, 1] = cos
    inner = inner.reshape(16, 256, 256)
    return tuple(
        np.ascontiguousarray(table).astype(ml_dtypes.bfloat16)
        for table in (outer, outer.T, inner, inner.transpose(0, 2, 1))
    )


def dot(a, b):
    return jnp.dot(a, b, preferred_element_type=F32)


def times(a, b, conj):
    ar, ai, br, bi = a[:128], a[128:], b[:128], b[128:]
    if conj:
        return jnp.concatenate([ar * br + ai * bi, ar * bi - ai * br], axis=0)
    return jnp.concatenate([ar * br - ai * bi, ar * bi + ai * br], axis=0)


def loop(n, body, unroll=1):
    def step(at, carry):
        body(at)
        return carry

    lax.fori_loop(0, n, step, 0, unroll=unroll)


def rows16(g):
    return pl.ds(pl.multiple_of(g * 16, 16), 16)


def kernel(
    q_in, k_in, v_in, h_in, w_in, g_in, p1_in, p1t_in, m_in, mt_in,
    block_out, query_out, mixed_out, filter_out, weight_out,
    q_v, k_v, v_v, h_v, p1, p1t, m_t, mt_t,
    mixed_send, mixed_recv, q_send, q_tile, g_tile, w_tile,
    conv_send, conv_tile, gg_tile, cg_send, cg_recv, gated, gated_t,
    qg_send, qg_recv, block_send, block_recv, wg_send, wg_recv,
    mg_send, mg_recv, f_send, f_recv, ws_send, ws_recv,
    s_buf, u_buf, u2_buf, h_spec, m_spec,
    lsem,
    mixed_s, mixed_r, q_s, q_r, g_s, g_r, w_s, w_r, conv_s, conv_r, cg_s, cg_r, qg_s, qg_r,
    block_s, block_r, wg_s, wg_r, mg_s, mg_r, f_s, f_r, fa_s, fa_r, ws_s, ws_r, wa_s, wa_r,
):
    dp = lax.axis_index("dp")
    me = lax.axis_index("ctx")
    i = lax.div(me, 4)
    j = lax.rem(me, 4)

    def ctx_peer(at):
        return lax.rem(me + at, 16)

    def dp_peer(at):
        return lax.rem(dp + at, 8)

    def i_peer(at):
        return lax.rem(i + at, 4)

    def j_peer(at):
        return lax.rem(j + at, 4)

    def remote(src, dst, s, r, to_dp, to_ctx):
        return pltpu.make_async_remote_copy(
            src_ref=src, dst_ref=dst, send_sem=s, recv_sem=r,
            device_id=(to_dp, to_ctx), device_id_type=MESH,
        )

    def mixed_copy(at):
        p = ctx_peer(at)
        return remote(mixed_send.at[p], mixed_recv.at[me], mixed_s.at[at], mixed_r.at[at], dp, p)

    def mg_copy(at):
        p = ctx_peer(at)
        return remote(mg_send.at[p], mg_recv.at[me], mg_s.at[at], mg_r.at[at], dp, p)

    def q_copy(at):
        p = j_peer(at)
        return remote(q_send.at[p], q_tile.at[:, j], q_s.at[at], q_r.at[at], dp, i * 4 + p)

    def g_copy(at):
        return remote(g_in, g_tile.at[j], g_s.at[at], g_r.at[at], dp, i * 4 + j_peer(at))

    def w_copy(at):
        return remote(w_in, w_tile.at[i], w_s.at[at], w_r.at[at], dp, i_peer(at) * 4 + j)

    def conv_copy(at):
        p = i_peer(at)
        return remote(
            conv_send.at[pl.ds(p * 4, 4)], conv_tile.at[i], conv_s.at[at], conv_r.at[at],
            dp, p * 4 + j,
        )

    def cg_copy(at):
        p = i_peer(at)
        return remote(
            cg_send.at[p], cg_recv.at[pl.ds(i * 4, 4)], cg_s.at[at], cg_r.at[at], dp, p * 4 + j
        )

    def qg_copy(at):
        p = j_peer(at)
        return remote(qg_send.at[p], qg_recv.at[j], qg_s.at[at], qg_r.at[at], dp, i * 4 + p)

    def block_copy(at):
        p = j_peer(at)
        return remote(
            block_send.at[p], block_recv.at[at], block_s.at[at], block_r.at[at], dp, i * 4 + p
        )

    def wg_copy(at):
        p = i_peer(at)
        return remote(wg_send.at[p], wg_recv.at[at], wg_s.at[at], wg_r.at[at], dp, p * 4 + j)

    def f_copy(at):
        p = dp_peer(at)
        return remote(f_send.at[p], f_recv.at[at], f_s.at[at], f_r.at[at], p, me)

    def fa_copy(at):
        p = dp_peer(at)
        return remote(filter_out.at[dp], filter_out.at[dp], fa_s.at[at], fa_r.at[at], p, me)

    def ws_copy(at):
        p = dp_peer(at)
        return remote(ws_send.at[p], ws_recv.at[at], ws_s.at[at], ws_r.at[at], p, me)

    def wa_copy(at):
        p = dp_peer(at)
        return remote(weight_out.at[dp], weight_out.at[dp], wa_s.at[at], wa_r.at[at], p, me)

    def each(copy, n, what):
        loop(n - 1, lambda at: getattr(copy(at + 1), what)())

    local = [
        pltpu.make_async_copy(src, dst, lsem.at[at])
        for at, (src, dst) in enumerate(
            [
                (k_in, k_v), (v_in, v_v), (q_in, q_v), (h_in, h_v), (p1_in, p1), (m_in, m_t),
                (mt_in, mt_t), (p1t_in, p1t), (g_in, g_tile.at[j]), (w_in, w_tile.at[i]),
            ]
        )
    ]
    for copy in local:
        copy.start()

    barrier = pltpu.get_barrier_semaphore()

    def greet_ctx(at):
        pl.semaphore_signal(
            barrier, inc=1, device_id=(dp, ctx_peer(at + 1)), device_id_type=MESH
        )

    def greet_dp(at):
        pl.semaphore_signal(barrier, inc=1, device_id=(dp_peer(at + 1), me), device_id_type=MESH)

    loop(15, greet_ctx)
    loop(7, greet_dp)

    local[0].wait()
    local[1].wait()
    for p in range(16):
        lanes = slice(p * 128, p * 128 + 128)
        mixed_send[p] = (k_v[:, lanes].astype(F32) * v_v[:, lanes].astype(F32)).astype(BF)
    local[2].wait()
    for p in range(16):
        q_send[p % 4, p // 4] = q_v[:, p * 128 : p * 128 + 128]

    pl.semaphore_wait(barrier, 22)
    each(mixed_copy, 16, "start")
    each(q_copy, 4, "start")
    each(w_copy, 4, "start")
    each(g_copy, 4, "start")
    mixed_recv[me] = mixed_send[me]
    q_tile[:, j] = q_send[j]

    def outer_step(x_ref):
        def body(g):
            x = x_ref[:, rows16(g), :].astype(BF).reshape(256, 128)
            s_buf[:, g] = dot(p1[...], x).reshape(16, 32, 128).astype(BF)

        loop(8, body, 2)

    def inner(k0):
        return dot(m_t[k0], s_buf[k0].reshape(256, 128))

    for at in range(3, 8):
        local[at].wait()
    outer_step(h_v)

    def filter_step(k0):
        h_spec[k0] = inner(k0)

    loop(16, filter_step, 2)

    each(mixed_copy, 16, "wait_recv")
    outer_step(mixed_recv)

    def conv_step(k0):
        spec = inner(k0)
        m_spec[k0] = spec
        y = times(h_spec[k0], spec, False).astype(BF)
        u_buf[k0] = dot(mt_t[k0], y).reshape(8, 32, 128).astype(BF)

    loop(16, conv_step, 4)

    def conv_last(g):
        y = dot(p1t[...], u_buf[:, g].reshape(512, 128)) * (1.0 / 2048.0)
        conv_send[:, rows16(g), :] = y.reshape(16, 16, 128).astype(BF)

    loop(8, conv_last, 2)
    each(conv_copy, 4, "start")
    conv_tile[i] = conv_send[pl.ds(i * 4, 4)]

    local[8].wait()
    local[9].wait()
    each(q_copy, 4, "wait_recv")
    each(w_copy, 4, "wait_recv")
    each(g_copy, 4, "wait_recv")
    for half in range(2):
        wide = lax.dot_general(
            g_tile[...].reshape(512, 2048),
            w_tile[2 * half : 2 * half + 2].reshape(256, 2048),
            (((1,), (1,)), ((), ())),
            preferred_element_type=F32,
        ).astype(BF)
        for at in range(2):
            part = 2 * half + at
            gg = wide[:, at * 128 : at * 128 + 128].reshape(4, 128, 128)
            gg_tile[part] = gg
            cg_send[part] = (gg.astype(F32) * q_tile[part].astype(F32)).astype(BF)
    each(cg_copy, 4, "start")
    cg_recv[pl.ds(i * 4, 4)] = cg_send[i]

    each(conv_copy, 4, "wait_recv")
    for part in range(4):
        conv = conv_tile[part].astype(F32)
        gate = (conv * q_tile[part].astype(F32)).astype(BF).reshape(512, 128)
        gated[:, part * 128 : part * 128 + 128] = gate
        gated_t[part * 128 : part * 128 + 128, :] = gate.astype(F32).T.astype(BF)
        qg = (conv * gg_tile[part].astype(F32)).astype(BF)
        for at in range(4):
            qg_send[at, part] = qg[at]
    each(qg_copy, 4, "start")
    qg_recv[j] = qg_send[j]

    def wg_step(n):
        lanes = pl.ds(pl.multiple_of(n * 256, 256), 256)
        y = dot(gated_t[...], g_tile[:, :, lanes].reshape(512, 256))
        wg_send[:, :, lanes] = y.astype(BF).reshape(4, 128, 256)

    loop(8, wg_step)
    each(wg_copy, 4, "start")

    def block_step(n):
        lanes = pl.ds(pl.multiple_of(n * 256, 256), 256)
        y = dot(gated[...], w_tile[:, :, lanes].reshape(512, 256))
        block_send[:, :, lanes] = y.astype(BF).reshape(4, 128, 256)

    loop(8, block_step)
    each(block_copy, 4, "start")

    each(cg_copy, 4, "wait_recv")
    outer_step(cg_recv)

    def back_step(k0):
        spec = inner(k0)
        y = jnp.concatenate(
            [times(h_spec[k0], spec, True), times(m_spec[k0], spec, True)], axis=1
        ).astype(BF)
        u2_buf[k0] = dot(mt_t[k0], y).reshape(8, 32, 256).astype(BF)

    loop(16, back_step, 4)

    def back_last(g):
        y = dot(p1t[...], u2_buf[:, g].reshape(512, 256)) * (1.0 / 2048.0)
        y = y.reshape(16, 16, 256).astype(BF)
        mg_send[:, rows16(g), :] = y[:, :, :128]
        f_send[:, :, rows16(g), :] = y[:, :, 128:].reshape(8, 2, 16, 128)

    loop(8, back_last, 2)
    each(mg_copy, 16, "start")
    each(f_copy, 8, "start")
    mg_recv[me] = mg_send[me]

    each(qg_copy, 4, "wait_recv")
    for p in range(16):
        query_out[:, p * 128 : p * 128 + 128] = qg_recv[p % 4, p // 4]

    each(wg_copy, 4, "wait_recv")

    def wsum_step(r):
        total = wg_send[i, rows16(r), :].astype(F32)
        for at in range(1, 4):
            total += wg_recv[at, rows16(r), :].astype(F32)
        ws_send[r] = total.astype(BF)

    loop(8, wsum_step)
    each(ws_copy, 8, "start")

    each(f_copy, 8, "wait_recv")
    total = f_send[dp].astype(F32)
    for at in range(1, 8):
        total += f_recv[at].astype(F32)
    filter_out[dp] = total.astype(BF)
    each(fa_copy, 8, "start")

    each(block_copy, 4, "wait_recv")

    def bsum_step(r):
        total = block_send[j, rows16(r), :].astype(F32)
        for at in range(1, 4):
            total += block_recv[at, rows16(r), :].astype(F32)
        block_out[rows16(r), :] = total.astype(BF)

    loop(8, bsum_step)

    each(ws_copy, 8, "wait_recv")
    total = ws_send[dp].astype(F32)
    for at in range(1, 8):
        total += ws_recv[at].astype(F32)
    weight_out[dp] = total.astype(BF)
    each(wa_copy, 8, "start")

    each(mg_copy, 16, "wait_recv")
    for p in range(16):
        mixed_out[:, p * 128 : p * 128 + 128] = mg_recv[p]

    each(fa_copy, 8, "wait_recv")
    each(wa_copy, 8, "wait_recv")
    each(mixed_copy, 16, "wait_send")
    each(mg_copy, 16, "wait_send")
    for copy in (q_copy, g_copy, w_copy, conv_copy, cg_copy, qg_copy, block_copy, wg_copy):
        each(copy, 4, "wait_send")
    for copy in (f_copy, fa_copy, ws_copy, wa_copy):
        each(copy, 8, "wait_send")


def shards(queries, key_proj, value_proj, filters, out_weight, out_grad):
    tables = make_tables()
    vm = pltpu.VMEM
    dma = pltpu.SemaphoreType.DMA
    scratch = [
        vm((128, 2048), BF), vm((128, 2048), BF), vm((128, 2048), BF), vm((16, 128, 128), F32),
        vm((512, 256), BF), vm((256, 512), BF), vm((16, 256, 256), BF), vm((16, 256, 256), BF),
        vm((16, 128, 128), BF), vm((16, 128, 128), BF),
        vm((4, 4, 128, 128), BF), vm((4, 4, 128, 128), BF),
        vm((4, 128, 2048), BF), vm((4, 128, 2048), BF),
        vm((16, 128, 128), BF), vm((4, 4, 128, 128), BF),
        vm((4, 4, 128, 128), BF),
        vm((4, 4, 128, 128), BF), vm((16, 128, 128), BF),
        vm((512, 512), BF), vm((512, 512), BF),
        vm((4, 4, 128, 128), BF), vm((4, 4, 128, 128), BF),
        vm((4, 128, 2048), BF), vm((4, 128, 2048), BF),
        vm((4, 128, 2048), BF), vm((4, 128, 2048), BF),
        vm((16, 128, 128), BF), vm((16, 128, 128), BF),
        vm((8, 2, 128, 128), BF), vm((8, 2, 128, 128), BF),
        vm((8, 16, 2048), BF), vm((8, 16, 2048), BF),
        vm((16, 8, 32, 128), BF), vm((16, 8, 32, 128), BF), vm((16, 8, 32, 256), BF),
        vm((16, 256, 128), F32), vm((16, 256, 128), F32),
        dma((10,)),
    ]
    for count in (16, 4, 4, 4, 4, 4, 4, 4, 4, 16, 8, 8, 8, 8):
        scratch += [dma((count,)), dma((count,))]
    anywhere = pl.BlockSpec(memory_space=pl.ANY)
    block, query, mixed, filt, weight = pl.pallas_call(
        kernel,
        name="hyena_block",
        out_shape=(
            jax.ShapeDtypeStruct((128, 2048), BF),
            jax.ShapeDtypeStruct((128, 2048), BF),
            jax.ShapeDtypeStruct((128, 2048), BF),
            jax.ShapeDtypeStruct((8, 2, 128, 128), BF),
            jax.ShapeDtypeStruct((8, 16, 2048), BF),
        ),
        in_specs=[anywhere] * 10,
        out_specs=[pl.BlockSpec(memory_space=pltpu.VMEM)] * 5,
        scratch_shapes=scratch,
        compiler_params=pltpu.CompilerParams(
            collective_id=0, has_side_effects=True, vmem_limit_bytes=58 << 20
        ),
    )(
        queries[0], key_proj[0], value_proj[0], filters.reshape(16, 128, 128), out_weight,
        out_grad[0], *tables,
    )
    wide = mixed.astype(F32)
    key_grad = (wide * value_proj[0].astype(F32)).astype(BF)
    value_grad = (wide * key_proj[0].astype(F32)).astype(BF)
    scale = 1.0 / math.sqrt(16384.0)
    return (
        block[None],
        query[None],
        key_grad[None],
        value_grad[None],
        filt.astype(F32).reshape(2048, 128) * scale,
        weight.astype(F32).reshape(128, 2048) * scale,
    )


def solution(mesh):
    rows = P("dp", "ctx", None)
    return jax.shard_map(
        shards,
        mesh=mesh,
        in_specs=(rows, rows, rows, P(None, "ctx"), P("ctx", None), rows),
        out_specs=(rows, rows, rows, rows, P(None, "ctx"), P("ctx", None)),
        check_vma=False,
    )
```

```python
import math

import jax
import jax.numpy as jnp
import ml_dtypes
import numpy as np
from jax import lax
from jax.experimental import pallas as pl
from jax.experimental.pallas import tpu as pltpu
from jax.sharding import PartitionSpec as P

MESH = pl.DeviceIdType.MESH
BF = jnp.bfloat16
F32 = jnp.float32


def make_tables():
    k0 = np.arange(16)
    t1 = np.arange(16)
    angle = 2.0 * np.pi * (k0[:, None] + 0.5) * t1[None, :] / 32.0
    outer = np.stack([np.cos(angle), -np.sin(angle)], axis=1)
    outer = np.einsum("krt,su->krstu", outer, np.eye(16)).reshape(512, 256)
    t0 = np.arange(128)
    k1 = np.arange(128)
    angle = (k0[:, None, None] + 0.5) * t0[None, None, :] / 4096.0 + (
        (k1[None, :, None] * t0[None, None, :]) % 128
    ) / 128.0
    cos = np.cos(2.0 * np.pi * angle).reshape(16, 128, 8, 16)
    sin = np.sin(2.0 * np.pi * angle).reshape(16, 128, 8, 16)
    inner = np.empty((16, 2, 128, 8, 2, 16))
    inner[:, 0, :, :, 0] = cos
    inner[:, 0, :, :, 1] = sin
    inner[:, 1, :, :, 0] = -sin
    inner[:, 1, :, :, 1] = cos
    inner = inner.reshape(16, 256, 256)
    return tuple(
        np.ascontiguousarray(table).astype(ml_dtypes.bfloat16)
        for table in (outer, outer.T, inner, inner.transpose(0, 2, 1))
    )


def dot(a, b):
    return jnp.dot(a, b, preferred_element_type=F32)


def times(a, b, conj):
    ar, ai, br, bi = a[:128], a[128:], b[:128], b[128:]
    if conj:
        return jnp.concatenate([ar * br + ai * bi, ar * bi - ai * br], axis=0)
    return jnp.concatenate([ar * br - ai * bi, ar * bi + ai * br], axis=0)


def loop(n, body, unroll=1):
    def step(at, carry):
        body(at)
        return carry

    lax.fori_loop(0, n, step, 0, unroll=unroll)


def rows16(g):
    return pl.ds(pl.multiple_of(g * 16, 16), 16)


def kernel(
    q_in, k_in, v_in, h_in, w_in, g_in, p1_in, p1t_in, m_in, mt_in,
    block_out, query_out, mixed_out, filter_out, weight_out,
    q_v, k_v, v_v, h_v, p1, p1t, m_t, mt_t,
    mixed_send, mixed_recv, q_send, q_tile, g_tile, w_tile,
    conv_send, conv_tile, gg_tile, cg_send, cg_recv, gated, gated_t,
    qg_send, qg_recv, block_send, block_core, block_red, block_far,
    wga_send, wga_recv, wgb_send, wgb_recv, wsa_send, wsa_recv, wsb_send, wsb_recv,
    wx_send, wx_recv, mg_send, mg_recv, f_send, f_recv, fx_send, fx_recv,
    s_buf, u_buf, u2_buf, h_spec, m_spec,
    lsem,
    mixed_s, mixed_r, mg_s, mg_r, q_s, q_r, w_s, w_r, wq_s, wq_r, wf_s, wf_r, conv_s, conv_r,
    cg_s, cg_r, qg_s, qg_r, wga_s, wga_r, wgb_s, wgb_r, wsa_s, wsa_r, wsb_s, wsb_r, wa_s, wa_r,
    f_s, f_r, fa_s, fa_r, g_s, g_r, block_s, block_r, x_s, x_r,
):
    dp = lax.axis_index("dp")
    me = lax.axis_index("ctx")
    i = lax.div(me, 4)
    j = lax.rem(me, 4)
    far = lax.div(j, 2)
    core = lax.rem(j, 2)
    z = lax.rem(dp, 4)
    j_core = far * 2 + (1 - core)
    j_far = (1 - far) * 2 + core
    near = lax.rem(dp + 4, 8)

    def ctx_peer(at):
        return lax.rem(me + at, 16)

    def z_peer(at):
        return lax.rem(z + at, 4)

    def to_z(at):
        return dp - z + z_peer(at)

    def i_peer(at):
        return lax.rem(i + at, 4)

    def j_peer(at):
        return lax.rem(j + at, 4)

    def remote(src, dst, s, r, to_dp, to_ctx):
        return pltpu.make_async_remote_copy(
            src_ref=src, dst_ref=dst, send_sem=s, recv_sem=r,
            device_id=(to_dp, to_ctx), device_id_type=MESH,
        )

    def mixed_copy(at):
        p = ctx_peer(at)
        return remote(mixed_send.at[p], mixed_recv.at[me], mixed_s.at[at], mixed_r.at[at], dp, p)

    def mg_copy(at):
        p = ctx_peer(at)
        return remote(mg_send.at[p], mg_recv.at[me], mg_s.at[at], mg_r.at[at], dp, p)

    def q_copy(at):
        p = j_peer(at)
        return remote(q_send.at[p], q_tile.at[:, j], q_s.at[at], q_r.at[at], dp, i * 4 + p)

    def g_core(at):
        rows = pl.ds(at * 64, 64)
        return remote(
            g_in.at[rows], g_tile.at[j, rows], g_s.at[at], g_r.at[at], dp, i * 4 + j_core
        )

    def g_far(at):
        rows = pl.ds(at * 64, 64)
        return remote(
            g_in.at[rows], g_tile.at[j, rows], g_s.at[2 + at], g_r.at[2 + at], dp, i * 4 + j_far
        )

    def g_pass(at):
        rows = pl.ds(at * 64, 64)
        ref = g_tile.at[j_far, rows]
        return remote(ref, ref, g_s.at[4 + at], g_r.at[4 + at], dp, i * 4 + j_core)

    def w_copy(at):
        rows = pl.ds(0, 64)
        return remote(
            w_in.at[rows], w_tile.at[i, rows], w_s.at[at], w_r.at[at], dp, i_peer(at) * 4 + j
        )

    def w_rows():
        return pl.ds(pl.multiple_of(64 + z * 16, 16), 16)

    def wq_copy(at):
        return remote(
            w_in.at[w_rows()], w_tile.at[i, w_rows()], wq_s.at[at], wq_r.at[at],
            dp, i_peer(at) * 4 + j,
        )

    def wf_copy(at):
        ref = w_tile.at[i_peer(1 + lax.rem(at, 3)), w_rows()]
        return remote(ref, ref, wf_s.at[at], wf_r.at[at], to_z(1 + lax.div(at, 3)), me)

    def conv_copy(at):
        p = i_peer(at)
        return remote(
            conv_send.at[pl.ds(p * 4, 4)], conv_tile.at[i], conv_s.at[at], conv_r.at[at],
            dp, p * 4 + j,
        )

    def cg_copy(at):
        p = i_peer(at)
        return remote(
            cg_send.at[p], cg_recv.at[pl.ds(i * 4, 4)], cg_s.at[at], cg_r.at[at], dp, p * 4 + j
        )

    def qg_copy(at):
        p = j_peer(at)
        return remote(qg_send.at[p], qg_recv.at[j], qg_s.at[at], qg_r.at[at], dp, i * 4 + p)

    def block_near(at):
        return remote(
            block_send.at[at * 2 + 1 - core], block_core.at[at], block_s.at[at], block_r.at[at],
            dp, i * 4 + j_core,
        )

    def block_cross(at):
        return remote(block_red, block_far, block_s.at[2], block_r.at[2], dp, i * 4 + j_far)

    def wga_copy(at):
        p = i_peer(at)
        return remote(wga_send.at[p], wga_recv.at[at], wga_s.at[at], wga_r.at[at], dp, p * 4 + j)

    def wgb_copy(at):
        rows = pl.ds(pl.multiple_of(z_peer(at) * 32, 32), 32)
        return remote(
            wgb_send.at[:, rows], wgb_recv.at[at], wgb_s.at[at], wgb_r.at[at], to_z(at), me
        )

    def wsa_copy(at):
        return remote(
            wsa_send.at[z_peer(at)], wsa_recv.at[at], wsa_s.at[at], wsa_r.at[at], to_z(at), me
        )

    def wsb_copy(at):
        p = i_peer(at)
        return remote(wsb_send.at[p], wsb_recv.at[at], wsb_s.at[at], wsb_r.at[at], dp, p * 4 + j)

    def wx_copy(at):
        return remote(wx_send, wx_recv, x_s.at[0], x_r.at[0], near, me)

    def wa_copy(at):
        return remote(weight_out.at[z], weight_out.at[z], wa_s.at[at], wa_r.at[at], to_z(at), me)

    def f_copy(at):
        return remote(f_send.at[z_peer(at)], f_recv.at[at], f_s.at[at], f_r.at[at], to_z(at), me)

    def fx_copy(at):
        return remote(fx_send, fx_recv, x_s.at[1], x_r.at[1], near, me)

    def fa_copy(at):
        return remote(filter_out.at[z], filter_out.at[z], fa_s.at[at], fa_r.at[at], to_z(at), me)

    def each(copy, n, what):
        loop(n - 1, lambda at: getattr(copy(at + 1), what)())

    local = [
        pltpu.make_async_copy(src, dst, lsem.at[at])
        for at, (src, dst) in enumerate(
            [
                (k_in, k_v), (v_in, v_v), (q_in, q_v), (h_in, h_v), (p1_in, p1), (m_in, m_t),
                (mt_in, mt_t), (p1t_in, p1t), (g_in, g_tile.at[j]), (w_in, w_tile.at[i]),
            ]
        )
    ]
    for copy in local:
        copy.start()

    barrier = pltpu.get_barrier_semaphore()

    def greet_ctx(at):
        pl.semaphore_signal(
            barrier, inc=1, device_id=(dp, ctx_peer(at + 1)), device_id_type=MESH
        )

    def greet_z(at):
        pl.semaphore_signal(barrier, inc=1, device_id=(to_z(at + 1), me), device_id_type=MESH)

    loop(15, greet_ctx)
    loop(3, greet_z)
    pl.semaphore_signal(barrier, inc=1, device_id=(near, me), device_id_type=MESH)

    local[0].wait()
    local[1].wait()
    for p in range(16):
        lanes = slice(p * 128, p * 128 + 128)
        mixed_send[p] = (k_v[:, lanes].astype(F32) * v_v[:, lanes].astype(F32)).astype(BF)
    local[2].wait()
    for p in range(16):
        q_send[p % 4, p // 4] = q_v[:, p * 128 : p * 128 + 128]

    pl.semaphore_wait(barrier, 19)
    each(mixed_copy, 16, "start")
    each(wq_copy, 4, "start")
    for at in range(2):
        g_far(at).start()
        g_core(at).start()
    each(q_copy, 4, "start")
    each(w_copy, 4, "start")
    mixed_recv[me] = mixed_send[me]
    q_tile[:, j] = q_send[j]

    def outer_step(x_ref):
        def body(g):
            x = x_ref[:, rows16(g), :].astype(BF).reshape(256, 128)
            s_buf[:, g] = dot(p1[...], x).reshape(16, 32, 128).astype(BF)

        loop(8, body, 2)

    def inner(k0):
        return dot(m_t[k0], s_buf[k0].reshape(256, 128))

    for at in range(3, 8):
        local[at].wait()
    outer_step(h_v)

    def filter_step(k0):
        h_spec[k0] = inner(k0)

    loop(16, filter_step, 2)

    each(wq_copy, 4, "wait_recv")
    loop(9, lambda at: wf_copy(at).start())

    each(mixed_copy, 16, "wait_recv")
    outer_step(mixed_recv)

    def conv_step(k0):
        spec = inner(k0)
        m_spec[k0] = spec
        y = times(h_spec[k0], spec, False).astype(BF)
        u_buf[k0] = dot(mt_t[k0], y).reshape(8, 32, 128).astype(BF)

    loop(16, conv_step, 4)

    def conv_last(g):
        y = dot(p1t[...], u_buf[:, g].reshape(512, 128)) * (1.0 / 2048.0)
        conv_send[:, rows16(g), :] = y.reshape(16, 16, 128).astype(BF)

    loop(8, conv_last, 2)
    each(conv_copy, 4, "start")
    conv_tile[i] = conv_send[pl.ds(i * 4, 4)]

    for at in range(2):
        g_far(at).wait_recv()
        g_pass(at).start()

    local[8].wait()
    local[9].wait()
    each(q_copy, 4, "wait_recv")
    each(w_copy, 4, "wait_recv")
    loop(9, lambda at: wf_copy(at).wait_recv())
    for at in range(2):
        g_core(at).wait_recv()
        g_pass(at).wait_recv()
    for half in range(2):
        wide = lax.dot_general(
            g_tile[...].reshape(512, 2048),
            w_tile[2 * half : 2 * half + 2].reshape(256, 2048),
            (((1,), (1,)), ((), ())),
            preferred_element_type=F32,
        ).astype(BF)
        for at in range(2):
            part = 2 * half + at
            gg = wide[:, at * 128 : at * 128 + 128].reshape(4, 128, 128)
            gg_tile[part] = gg
            cg_send[part] = (gg.astype(F32) * q_tile[part].astype(F32)).astype(BF)
    each(cg_copy, 4, "start")
    cg_recv[pl.ds(i * 4, 4)] = cg_send[i]

    each(conv_copy, 4, "wait_recv")
    for part in range(4):
        conv = conv_tile[part].astype(F32)
        gate = (conv * q_tile[part].astype(F32)).astype(BF).reshape(512, 128)
        gated[:, part * 128 : part * 128 + 128] = gate
        gated_t[part * 128 : part * 128 + 128, :] = gate.astype(F32).T.astype(BF)
        qg = (conv * gg_tile[part].astype(F32)).astype(BF)
        for at in range(4):
            qg_send[at, part] = qg[at]
    each(qg_copy, 4, "start")
    qg_recv[j] = qg_send[j]

    def block_step(n):
        lanes = pl.ds(pl.multiple_of(n * 256, 256), 256)
        y = dot(gated[...], w_tile[:, :, lanes].reshape(512, 256))
        block_send[:, :, lanes] = y.astype(BF).reshape(4, 128, 256)

    loop(8, block_step)
    for at in range(2):
        block_near(at).start()

    def wg_step(out, n, first):
        lanes = pl.ds(pl.multiple_of(n * 256, 256), 256)
        cols = pl.ds(pl.multiple_of(first + n * 256, 256), 256)
        y = dot(gated_t[...], g_tile[:, :, cols].reshape(512, 256))
        out[:, :, lanes] = y.astype(BF).reshape(4, 128, 256)

    loop(4, lambda n: wg_step(wga_send, n, 0))
    each(wga_copy, 4, "start")
    loop(4, lambda n: wg_step(wgb_send, n, 1024))
    each(wgb_copy, 4, "start")

    for at in range(2):
        block_near(at).wait_recv()

    def bred_step(r):
        block_red[rows16(r), :] = (
            block_send[j_far, rows16(r), :].astype(F32)
            + block_core[1 - far, rows16(r), :].astype(F32)
        ).astype(BF)

    loop(8, bred_step)
    block_cross(0).start()

    each(cg_copy, 4, "wait_recv")
    outer_step(cg_recv)

    def back_step(k0):
        spec = inner(k0)
        y = jnp.concatenate(
            [times(h_spec[k0], spec, True), times(m_spec[k0], spec, True)], axis=1
        ).astype(BF)
        u2_buf[k0] = dot(mt_t[k0], y).reshape(8, 32, 256).astype(BF)

    loop(16, back_step, 4)

    def back_last(g):
        y = dot(p1t[...], u2_buf[:, g].reshape(512, 256)) * (1.0 / 2048.0)
        y = y.reshape(16, 16, 256).astype(BF)
        mg_send[:, rows16(g), :] = y[:, :, :128]
        f_send[:, :, rows16(g), :] = y[:, :, 128:].reshape(4, 4, 16, 128)

    loop(8, back_last, 2)
    each(mg_copy, 16, "start")
    each(f_copy, 4, "start")
    mg_recv[me] = mg_send[me]

    each(qg_copy, 4, "wait_recv")
    for p in range(16):
        query_out[:, p * 128 : p * 128 + 128] = qg_recv[p % 4, p // 4]

    each(wga_copy, 4, "wait_recv")

    def suma_step(r):
        total = wga_send[i, rows16(r), :].astype(F32)
        for at in range(1, 4):
            total += wga_recv[at, rows16(r), :].astype(F32)
        wsa_send[lax.div(r, 2), rows16(lax.rem(r, 2)), :] = total.astype(BF)

    loop(8, suma_step)
    each(wsa_copy, 4, "start")
    each(wgb_copy, 4, "wait_recv")

    def sumb_step(r):
        total = wgb_send[r, pl.ds(pl.multiple_of(z * 32, 32), 32), :].astype(F32)
        for at in range(1, 4):
            total += wgb_recv[at, r].astype(F32)
        wsb_send[r] = total.astype(BF)

    loop(4, sumb_step)
    each(wsb_copy, 4, "start")

    each(f_copy, 4, "wait_recv")
    total = f_send[z].astype(F32)
    for at in range(1, 4):
        total += f_recv[at].astype(F32)
    fx_send[...] = total.astype(BF)
    fx_copy(0).start()

    each(wsa_copy, 4, "wait_recv")
    total = wsa_send[z].astype(F32)
    for at in range(1, 4):
        total += wsa_recv[at].astype(F32)
    wx_send[:, :1024] = total.astype(BF)
    each(wsb_copy, 4, "wait_recv")
    total = wsb_send[i].astype(F32)
    for at in range(1, 4):
        total += wsb_recv[at].astype(F32)
    wx_send[:, 1024:] = total.astype(BF)
    wx_copy(0).start()

    fx_copy(0).wait_recv()
    filter_out[z] = (fx_send[...].astype(F32) + fx_recv[...].astype(F32)).astype(BF)
    each(fa_copy, 4, "start")

    block_cross(0).wait_recv()

    def bsum_step(r):
        block_out[rows16(r), :] = (
            block_send[j, rows16(r), :].astype(F32)
            + block_core[far, rows16(r), :].astype(F32)
            + block_far[rows16(r), :].astype(F32)
        ).astype(BF)

    loop(8, bsum_step)

    wx_copy(0).wait_recv()
    weight_out[z] = (wx_send[...].astype(F32) + wx_recv[...].astype(F32)).astype(BF)
    each(wa_copy, 4, "start")

    each(mg_copy, 16, "wait_recv")
    for p in range(16):
        mixed_out[:, p * 128 : p * 128 + 128] = mg_recv[p]

    each(fa_copy, 4, "wait_recv")
    each(wa_copy, 4, "wait_recv")
    each(mixed_copy, 16, "wait_send")
    each(mg_copy, 16, "wait_send")
    for copy in (
        q_copy, w_copy, wq_copy, conv_copy, cg_copy, qg_copy, wga_copy, wgb_copy, wsa_copy,
        wsb_copy, wa_copy, f_copy, fa_copy,
    ):
        each(copy, 4, "wait_send")
    loop(9, lambda at: wf_copy(at).wait_send())
    for at in range(2):
        for copy in (g_core, g_far, g_pass, block_near):
            copy(at).wait_send()
    for copy in (block_cross, wx_copy, fx_copy):
        copy(0).wait_send()


def shards(queries, key_proj, value_proj, filters, out_weight, out_grad):
    tables = make_tables()
    vm = pltpu.VMEM
    dma = pltpu.SemaphoreType.DMA
    scratch = [
        vm((128, 2048), BF), vm((128, 2048), BF), vm((128, 2048), BF), vm((16, 128, 128), F32),
        vm((512, 256), BF), vm((256, 512), BF), vm((16, 256, 256), BF), vm((16, 256, 256), BF),
        vm((16, 128, 128), BF), vm((16, 128, 128), BF),
        vm((4, 4, 128, 128), BF), vm((4, 4, 128, 128), BF),
        vm((4, 128, 2048), BF), vm((4, 128, 2048), BF),
        vm((16, 128, 128), BF), vm((4, 4, 128, 128), BF),
        vm((4, 4, 128, 128), BF),
        vm((4, 4, 128, 128), BF), vm((16, 128, 128), BF),
        vm((512, 512), BF), vm((512, 512), BF),
        vm((4, 4, 128, 128), BF), vm((4, 4, 128, 128), BF),
        vm((4, 128, 2048), BF), vm((2, 128, 2048), BF),
        vm((128, 2048), BF), vm((128, 2048), BF),
        vm((4, 128, 1024), BF), vm((4, 128, 1024), BF),
        vm((4, 128, 1024), BF), vm((4, 4, 32, 1024), BF),
        vm((4, 32, 1024), BF), vm((4, 32, 1024), BF),
        vm((4, 32, 1024), BF), vm((4, 32, 1024), BF),
        vm((32, 2048), BF), vm((32, 2048), BF),
        vm((16, 128, 128), BF), vm((16, 128, 128), BF),
        vm((4, 4, 128, 128), BF), vm((4, 4, 128, 128), BF),
        vm((4, 128, 128), BF), vm((4, 128, 128), BF),
        vm((16, 8, 32, 128), BF), vm((16, 8, 32, 128), BF), vm((16, 8, 32, 256), BF),
        vm((16, 256, 128), F32), vm((16, 256, 128), F32),
        dma((10,)),
    ]
    for count in (16, 16, 4, 4, 4, 9, 4, 4, 4, 4, 4, 4, 4, 4, 4, 4, 6, 3, 2):
        scratch += [dma((count,)), dma((count,))]
    anywhere = pl.BlockSpec(memory_space=pl.ANY)
    block, query, mixed, filt, weight = pl.pallas_call(
        kernel,
        name="hyena_block",
        out_shape=(
            jax.ShapeDtypeStruct((128, 2048), BF),
            jax.ShapeDtypeStruct((128, 2048), BF),
            jax.ShapeDtypeStruct((128, 2048), BF),
            jax.ShapeDtypeStruct((4, 4, 128, 128), BF),
            jax.ShapeDtypeStruct((4, 32, 2048), BF),
        ),
        in_specs=[anywhere] * 10,
        out_specs=[pl.BlockSpec(memory_space=pltpu.VMEM)] * 5,
        scratch_shapes=scratch,
        compiler_params=pltpu.CompilerParams(
            collective_id=0, has_side_effects=True, vmem_limit_bytes=58 << 20
        ),
    )(
        queries[0], key_proj[0], value_proj[0], filters.reshape(16, 128, 128), out_weight,
        out_grad[0], *tables,
    )
    wide = mixed.astype(F32)
    key_grad = (wide * value_proj[0].astype(F32)).astype(BF)
    value_grad = (wide * key_proj[0].astype(F32)).astype(BF)
    scale = 1.0 / math.sqrt(16384.0)
    return (
        block[None],
        query[None],
        key_grad[None],
        value_grad[None],
        filt.astype(F32).reshape(2048, 128) * scale,
        weight.astype(F32).reshape(128, 2048) * scale,
    )


def solution(mesh):
    rows = P("dp", "ctx", None)
    return jax.shard_map(
        shards,
        mesh=mesh,
        in_specs=(rows, rows, rows, P(None, "ctx"), P("ctx", None), rows),
        out_specs=(rows, rows, rows, rows, P(None, "ctx"), P("ctx", None)),
        check_vma=False,
    )
```

```python
import math

import jax
import jax.numpy as jnp
import ml_dtypes
import numpy as np
from jax import lax
from jax.experimental import pallas as pl
from jax.experimental.pallas import tpu as pltpu
from jax.sharding import PartitionSpec as P

MESH = pl.DeviceIdType.MESH
BF = jnp.bfloat16
F32 = jnp.float32


def make_tables():
    k0 = np.arange(16)
    t1 = np.arange(16)
    angle = 2.0 * np.pi * (k0[:, None] + 0.5) * t1[None, :] / 32.0
    outer = np.stack([np.cos(angle), -np.sin(angle)], axis=1)
    outer = np.einsum("krt,su->krstu", outer, np.eye(16)).reshape(512, 256)
    t0 = np.arange(128)
    k1 = np.arange(128)
    angle = (k0[:, None, None] + 0.5) * t0[None, None, :] / 4096.0 + (
        (k1[None, :, None] * t0[None, None, :]) % 128
    ) / 128.0
    cos = np.cos(2.0 * np.pi * angle).reshape(16, 128, 8, 16)
    sin = np.sin(2.0 * np.pi * angle).reshape(16, 128, 8, 16)
    inner = np.empty((16, 2, 128, 8, 2, 16))
    inner[:, 0, :, :, 0] = cos
    inner[:, 0, :, :, 1] = sin
    inner[:, 1, :, :, 0] = -sin
    inner[:, 1, :, :, 1] = cos
    inner = inner.reshape(16, 256, 256)
    return tuple(
        np.ascontiguousarray(table).astype(ml_dtypes.bfloat16)
        for table in (outer, outer.T, inner, inner.transpose(0, 2, 1))
    )


def dot(a, b):
    return jnp.dot(a, b, preferred_element_type=F32)


def times(a, b, conj):
    ar, ai, br, bi = a[:128], a[128:], b[:128], b[128:]
    if conj:
        return jnp.concatenate([ar * br + ai * bi, ar * bi - ai * br], axis=0)
    return jnp.concatenate([ar * br - ai * bi, ar * bi + ai * br], axis=0)


def loop(n, body, unroll=1):
    def step(at, carry):
        body(at)
        return carry

    lax.fori_loop(0, n, step, 0, unroll=unroll)


def rows16(g):
    return pl.ds(pl.multiple_of(g * 16, 16), 16)


def kernel(
    q_in, k_in, v_in, h_in, w_in, g_in, p1_in, p1t_in, m_in, mt_in,
    block_out, query_out, key_out, value_out, filter_out, weight_out,
    q_v, k_v, v_v, h_v, p1, p1t, m_t, mt_t,
    mixed_send, mixed_recv, q_send, q_tile, g_tile, w_tile,
    conv_send, conv_tile, gg_tile, cg_send, cg_recv, gated, gated_t,
    qg_send, qg_recv, block_send, block_core, block_red, block_far,
    wga_send, wga_recv, wgb_send, wgb_recv, wsa_send, wsa_recv, wsb_send, wsb_recv,
    wx_send, wx_recv, mg_send, mg_recv, f_send, f_recv, fx_send, fx_recv,
    s_buf, u_buf, u2_buf, h_spec, m_spec,
    f_total, w_total, block_v, key_v, value_v, lsem, osem,
    mixed_s, mixed_r, mg_s, mg_r, q_s, q_r, w_s, w_r, wq_s, wq_r, wf_s, wf_r, conv_s, conv_r,
    cg_s, cg_r, qg_s, qg_r, wga_s, wga_r, wgb_s, wgb_r, wsa_s, wsa_r, wsb_s, wsb_r, wa_s, wa_r,
    f_s, f_r, fa_s, fa_r, g_s, g_r, block_s, block_r, x_s, x_r,
):
    dp = lax.axis_index("dp")
    me = lax.axis_index("ctx")
    i = lax.div(me, 4)
    j = lax.rem(me, 4)
    far = lax.div(j, 2)
    core = lax.rem(j, 2)
    z = lax.rem(dp, 4)
    j_core = far * 2 + (1 - core)
    j_far = (1 - far) * 2 + core
    near = lax.rem(dp + 4, 8)

    def ctx_peer(at):
        return lax.rem(me + at, 16)

    def z_peer(at):
        return lax.rem(z + at, 4)

    def to_z(at):
        return dp - z + z_peer(at)

    def i_peer(at):
        return lax.rem(i + at, 4)

    def j_peer(at):
        return lax.rem(j + at, 4)

    def remote(src, dst, s, r, to_dp, to_ctx):
        return pltpu.make_async_remote_copy(
            src_ref=src, dst_ref=dst, send_sem=s, recv_sem=r,
            device_id=(to_dp, to_ctx), device_id_type=MESH,
        )

    def mixed_copy(at):
        p = ctx_peer(at)
        return remote(mixed_send.at[p], mixed_recv.at[me], mixed_s.at[at], mixed_r.at[at], dp, p)

    def mg_copy(at):
        p = ctx_peer(at)
        return remote(mg_send.at[p], mg_recv.at[me], mg_s.at[at], mg_r.at[at], dp, p)

    def q_copy(at):
        p = j_peer(at)
        return remote(q_send.at[p], q_tile.at[:, j], q_s.at[at], q_r.at[at], dp, i * 4 + p)

    def g_core(at):
        rows = pl.ds(at * 64, 64)
        return remote(
            g_in.at[rows], g_tile.at[j, rows], g_s.at[at], g_r.at[at], dp, i * 4 + j_core
        )

    def g_far(at):
        rows = pl.ds(at * 64, 64)
        return remote(
            g_in.at[rows], g_tile.at[j, rows], g_s.at[2 + at], g_r.at[2 + at], dp, i * 4 + j_far
        )

    def g_pass(at):
        rows = pl.ds(at * 64, 64)
        ref = g_tile.at[j_far, rows]
        return remote(ref, ref, g_s.at[4 + at], g_r.at[4 + at], dp, i * 4 + j_core)

    def w_copy(at):
        rows = pl.ds(0, 64)
        return remote(
            w_in.at[rows], w_tile.at[i, rows], w_s.at[at], w_r.at[at], dp, i_peer(at) * 4 + j
        )

    def w_rows():
        return pl.ds(pl.multiple_of(64 + z * 16, 16), 16)

    def wq_copy(at):
        return remote(
            w_in.at[w_rows()], w_tile.at[i, w_rows()], wq_s.at[at], wq_r.at[at],
            dp, i_peer(at) * 4 + j,
        )

    def wf_copy(at):
        ref = w_tile.at[i_peer(1 + lax.rem(at, 3)), w_rows()]
        return remote(ref, ref, wf_s.at[at], wf_r.at[at], to_z(1 + lax.div(at, 3)), me)

    def conv_copy(at):
        p = i_peer(at)
        return remote(
            conv_send.at[pl.ds(p * 4, 4)], conv_tile.at[i], conv_s.at[at], conv_r.at[at],
            dp, p * 4 + j,
        )

    def cg_half(at, side, first):
        p = i_peer(at)
        return remote(
            cg_send.at[p, pl.ds(side * 2, 2)], cg_recv.at[pl.ds(i * 4 + side * 2, 2)],
            cg_s.at[first + at], cg_r.at[first + at], dp, p * 4 + j,
        )

    def cg_mine(at):
        return cg_half(at, far, 0)

    def cg_other(at):
        return cg_half(at, 1 - far, 4)

    def qg_copy(at):
        p = j_peer(at)
        return remote(qg_send.at[p], qg_recv.at[j], qg_s.at[at], qg_r.at[at], dp, i * 4 + p)

    def block_near(at):
        return remote(
            block_send.at[at * 2 + 1 - core], block_core.at[at], block_s.at[at], block_r.at[at],
            dp, i * 4 + j_core,
        )

    def block_cross(at):
        return remote(block_red, block_far, block_s.at[2], block_r.at[2], dp, i * 4 + j_far)

    def wga_copy(at):
        p = i_peer(at)
        return remote(wga_send.at[p], wga_recv.at[at], wga_s.at[at], wga_r.at[at], dp, p * 4 + j)

    def wgb_copy(at):
        rows = pl.ds(pl.multiple_of(z_peer(at) * 32, 32), 32)
        return remote(
            wgb_send.at[:, rows], wgb_recv.at[at], wgb_s.at[at], wgb_r.at[at], to_z(at), me
        )

    def wsa_copy(at):
        return remote(
            wsa_send.at[z_peer(at)], wsa_recv.at[at], wsa_s.at[at], wsa_r.at[at], to_z(at), me
        )

    def wsb_copy(at):
        p = i_peer(at)
        return remote(wsb_send.at[p], wsb_recv.at[at], wsb_s.at[at], wsb_r.at[at], dp, p * 4 + j)

    def wx_copy(at):
        return remote(wx_send, wx_recv, x_s.at[0], x_r.at[0], near, me)

    def wa_copy(at):
        return remote(w_total.at[z], w_total.at[z], wa_s.at[at], wa_r.at[at], to_z(at), me)

    def f_copy(at):
        return remote(f_send.at[z_peer(at)], f_recv.at[at], f_s.at[at], f_r.at[at], to_z(at), me)

    def fx_copy(at):
        return remote(fx_send, fx_recv, x_s.at[1], x_r.at[1], near, me)

    def fa_copy(at):
        return remote(f_total.at[z], f_total.at[z], fa_s.at[at], fa_r.at[at], to_z(at), me)

    def leave(at, src, dst):
        return pltpu.make_async_copy(src, dst, osem.at[at])

    def each(copy, n, what):
        loop(n - 1, lambda at: getattr(copy(at + 1), what)())

    local = [
        pltpu.make_async_copy(src, dst, lsem.at[at])
        for at, (src, dst) in enumerate(
            [
                (k_in, k_v), (v_in, v_v), (q_in, q_v), (h_in, h_v), (p1_in, p1), (m_in, m_t),
                (mt_in, mt_t), (p1t_in, p1t), (g_in, g_tile.at[j]), (w_in, w_tile.at[i]),
            ]
        )
    ]
    local[0].start()
    local[1].start()

    barrier = pltpu.get_barrier_semaphore()

    def greet_ctx(at):
        pl.semaphore_signal(
            barrier, inc=1, device_id=(dp, ctx_peer(at + 1)), device_id_type=MESH
        )

    def greet_z(at):
        pl.semaphore_signal(barrier, inc=1, device_id=(to_z(at + 1), me), device_id_type=MESH)

    loop(15, greet_ctx)
    loop(3, greet_z)
    pl.semaphore_signal(barrier, inc=1, device_id=(near, me), device_id_type=MESH)

    local[0].wait()
    local[1].wait()
    for at in range(2, 10):
        local[at].start()
    for p in range(16):
        lanes = slice(p * 128, p * 128 + 128)
        mixed_send[p] = (k_v[:, lanes].astype(F32) * v_v[:, lanes].astype(F32)).astype(BF)
    local[2].wait()
    for p in range(16):
        q_send[p % 4, p // 4] = q_v[:, p * 128 : p * 128 + 128]

    pl.semaphore_wait(barrier, 19)
    each(mixed_copy, 16, "start")
    each(wq_copy, 4, "start")
    mixed_recv[me] = mixed_send[me]
    q_tile[:, j] = q_send[j]

    def outer_step(x_ref):
        def body(g):
            x = x_ref[:, rows16(g), :].astype(BF).reshape(256, 128)
            s_buf[:, g] = dot(p1[...], x).reshape(16, 32, 128).astype(BF)

        loop(8, body, 2)

    def inner(k0):
        return dot(m_t[k0], s_buf[k0].reshape(256, 128))

    for at in range(3, 8):
        local[at].wait()
    outer_step(h_v)

    def filter_step(k0):
        h_spec[k0] = inner(k0)

    loop(16, filter_step, 2)

    for at in range(2):
        g_far(at).start()
        g_core(at).start()
    each(w_copy, 4, "start")
    each(q_copy, 4, "start")
    each(wq_copy, 4, "wait_recv")
    loop(9, lambda at: wf_copy(at).start())

    each(mixed_copy, 16, "wait_recv")
    outer_step(mixed_recv)

    def conv_step(k0):
        spec = inner(k0)
        m_spec[k0] = spec
        y = times(h_spec[k0], spec, False).astype(BF)
        u_buf[k0] = dot(mt_t[k0], y).reshape(8, 32, 128).astype(BF)

    loop(16, conv_step, 4)

    def conv_last(g):
        y = dot(p1t[...], u_buf[:, g].reshape(512, 128)) * (1.0 / 2048.0)
        conv_send[:, rows16(g), :] = y.reshape(16, 16, 128).astype(BF)

    loop(8, conv_last, 2)
    each(conv_copy, 4, "start")
    conv_tile[i] = conv_send[pl.ds(i * 4, 4)]

    for at in range(2):
        g_far(at).wait_recv()
        g_pass(at).start()

    local[8].wait()
    local[9].wait()

    def grad_rows(side):
        rows = pl.ds(side * 2, 2)
        for half in range(2):
            wide = lax.dot_general(
                g_tile[rows].reshape(256, 2048),
                w_tile[2 * half : 2 * half + 2].reshape(256, 2048),
                (((1,), (1,)), ((), ())),
                preferred_element_type=F32,
            ).astype(BF)
            for at in range(2):
                part = 2 * half + at
                gg = wide[:, at * 128 : at * 128 + 128].reshape(2, 128, 128)
                gg_tile[part, rows] = gg
                cg_send[part, rows] = (
                    gg.astype(F32) * q_tile[part, rows].astype(F32)
                ).astype(BF)

    each(w_copy, 4, "wait_recv")
    loop(9, lambda at: wf_copy(at).wait_recv())
    for at in range(2):
        g_core(at).wait_recv()
    each(q_copy, 4, "wait_recv")
    grad_rows(far)
    each(cg_mine, 4, "start")
    for at in range(2):
        g_pass(at).wait_recv()
    grad_rows(1 - far)
    each(cg_other, 4, "start")
    cg_recv[pl.ds(i * 4, 4)] = cg_send[i]

    each(conv_copy, 4, "wait_recv")
    for part in range(4):
        conv = conv_tile[part].astype(F32)
        gate = (conv * q_tile[part].astype(F32)).astype(BF).reshape(512, 128)
        gated[:, part * 128 : part * 128 + 128] = gate
        gated_t[part * 128 : part * 128 + 128, :] = gate.astype(F32).T.astype(BF)
        qg = (conv * gg_tile[part].astype(F32)).astype(BF)
        for at in range(4):
            qg_send[at, part] = qg[at]
    each(qg_copy, 4, "start")
    qg_recv[j] = qg_send[j]

    def block_step(n):
        lanes = pl.ds(pl.multiple_of(n * 256, 256), 256)
        y = dot(gated[...], w_tile[:, :, lanes].reshape(512, 256))
        block_send[:, :, lanes] = y.astype(BF).reshape(4, 128, 256)

    loop(8, block_step)
    block_near(1 - far).start()
    block_near(far).start()

    def wg_step(out, n, first):
        lanes = pl.ds(pl.multiple_of(n * 256, 256), 256)
        cols = pl.ds(pl.multiple_of(first + n * 256, 256), 256)
        y = dot(gated_t[...], g_tile[:, :, cols].reshape(512, 256))
        out[:, :, lanes] = y.astype(BF).reshape(4, 128, 256)

    loop(4, lambda n: wg_step(wga_send, n, 0))
    each(wga_copy, 4, "start")
    loop(4, lambda n: wg_step(wgb_send, n, 1024))
    each(wgb_copy, 4, "start")

    block_near(1 - far).wait_recv()

    def bred_step(r):
        block_red[rows16(r), :] = (
            block_send[j_far, rows16(r), :].astype(F32)
            + block_core[1 - far, rows16(r), :].astype(F32)
        ).astype(BF)

    loop(8, bred_step)
    block_cross(0).start()

    each(cg_mine, 4, "wait_recv")
    each(cg_other, 4, "wait_recv")
    outer_step(cg_recv)

    def back_step(k0):
        spec = inner(k0)
        y = jnp.concatenate(
            [times(h_spec[k0], spec, True), times(m_spec[k0], spec, True)], axis=1
        ).astype(BF)
        u2_buf[k0] = dot(mt_t[k0], y).reshape(8, 32, 256).astype(BF)

    loop(16, back_step, 4)

    def back_last(g):
        y = dot(p1t[...], u2_buf[:, g].reshape(512, 256)) * (1.0 / 2048.0)
        y = y.reshape(16, 16, 256).astype(BF)
        mg_send[:, rows16(g), :] = y[:, :, :128]
        f_send[:, :, rows16(g), :] = y[:, :, 128:].reshape(4, 4, 16, 128)

    loop(8, back_last, 2)
    each(f_copy, 4, "start")
    each(mg_copy, 16, "start")
    mg_recv[me] = mg_send[me]

    each(qg_copy, 4, "wait_recv")
    for p in range(16):
        q_v[:, p * 128 : p * 128 + 128] = qg_recv[p % 4, p // 4]
    leave(0, q_v, query_out).start()

    each(wga_copy, 4, "wait_recv")

    def suma_step(r):
        total = wga_send[i, rows16(r), :].astype(F32)
        for at in range(1, 4):
            total += wga_recv[at, rows16(r), :].astype(F32)
        wsa_send[lax.div(r, 2), rows16(lax.rem(r, 2)), :] = total.astype(BF)

    loop(8, suma_step)
    each(wsa_copy, 4, "start")
    each(wgb_copy, 4, "wait_recv")

    def sumb_step(r):
        total = wgb_send[r, pl.ds(pl.multiple_of(z * 32, 32), 32), :].astype(F32)
        for at in range(1, 4):
            total += wgb_recv[at, r].astype(F32)
        wsb_send[r] = total.astype(BF)

    loop(4, sumb_step)
    each(wsb_copy, 4, "start")

    each(f_copy, 4, "wait_recv")
    total = f_send[z].astype(F32)
    for at in range(1, 4):
        total += f_recv[at].astype(F32)
    fx_send[...] = total.astype(BF)
    fx_copy(0).start()

    each(wsa_copy, 4, "wait_recv")
    total = wsa_send[z].astype(F32)
    for at in range(1, 4):
        total += wsa_recv[at].astype(F32)
    wx_send[:, :1024] = total.astype(BF)
    each(wsb_copy, 4, "wait_recv")
    total = wsb_send[i].astype(F32)
    for at in range(1, 4):
        total += wsb_recv[at].astype(F32)
    wx_send[:, 1024:] = total.astype(BF)
    wx_copy(0).start()

    fx_copy(0).wait_recv()
    f_total[z] = (fx_send[...].astype(F32) + fx_recv[...].astype(F32)).astype(BF)
    each(fa_copy, 4, "start")

    block_near(far).wait_recv()
    block_cross(0).wait_recv()

    def bsum_step(r):
        block_v[rows16(r), :] = (
            block_send[j, rows16(r), :].astype(F32)
            + block_core[far, rows16(r), :].astype(F32)
            + block_far[rows16(r), :].astype(F32)
        ).astype(BF)

    loop(8, bsum_step)
    leave(1, block_v, block_out).start()

    wx_copy(0).wait_recv()
    w_total[z] = (wx_send[...].astype(F32) + wx_recv[...].astype(F32)).astype(BF)
    each(wa_copy, 4, "start")

    each(mg_copy, 16, "wait_recv")
    for p in range(16):
        lanes = slice(p * 128, p * 128 + 128)
        mg = mg_recv[p].astype(F32)
        key_v[:, lanes] = (mg * v_v[:, lanes].astype(F32)).astype(BF)
        value_v[:, lanes] = (mg * k_v[:, lanes].astype(F32)).astype(BF)
    leave(2, key_v, key_out).start()
    leave(5, value_v, value_out).start()

    each(fa_copy, 4, "wait_recv")
    leave(3, f_total, filter_out).start()
    each(wa_copy, 4, "wait_recv")
    leave(4, w_total, weight_out).start()
    each(mixed_copy, 16, "wait_send")
    each(mg_copy, 16, "wait_send")
    for copy in (
        q_copy, w_copy, wq_copy, conv_copy, cg_mine, cg_other, qg_copy, wga_copy, wgb_copy, wsa_copy,
        wsb_copy, wa_copy, f_copy, fa_copy,
    ):
        each(copy, 4, "wait_send")
    loop(9, lambda at: wf_copy(at).wait_send())
    for at in range(2):
        for copy in (g_core, g_far, g_pass, block_near):
            copy(at).wait_send()
    for copy in (block_cross, wx_copy, fx_copy):
        copy(0).wait_send()
    for at, (src, dst) in enumerate(
        [(q_v, query_out), (block_v, block_out), (key_v, key_out), (f_total, filter_out),
         (w_total, weight_out), (value_v, value_out)]
    ):
        leave(at, src, dst).wait()


def finish(
    block_in, query_in, key_in, value_in, filter_in, weight_in,
    block_out, query_out, key_out, value_out, filter_out, weight_out,
    f_v, w_v, f_wide, w_wide, rows, sem,
):
    scale = 1.0 / math.sqrt(16384.0)

    def move(at, src, dst):
        copy = pltpu.make_async_copy(src, dst, sem.at[at])
        copy.start()
        return copy

    loads = [
        move(at, src, dst)
        for at, (src, dst) in enumerate(
            [
                (filter_in, f_v), (weight_in, w_v), (block_in, rows.at[0]),
                (query_in, rows.at[1]), (key_in, rows.at[2]), (value_in, rows.at[3]),
            ]
        )
    ]
    loads[0].wait()
    f_wide[...] = f_v[...].astype(F32) * scale
    moves = [move(6, f_wide, filter_out)]
    loads[1].wait()
    w_wide[...] = w_v[...].astype(F32) * scale
    moves.append(move(7, w_wide, weight_out))
    for at, out in enumerate((block_out, query_out, key_out, value_out)):
        loads[2 + at].wait()
        moves.append(move(8 + at, rows.at[at], out))
    for copy in moves:
        copy.wait()


def shards(queries, key_proj, value_proj, filters, out_weight, out_grad):
    tables = make_tables()
    vm = pltpu.VMEM
    dma = pltpu.SemaphoreType.DMA
    scratch = [
        vm((128, 2048), BF), vm((128, 2048), BF), vm((128, 2048), BF), vm((16, 128, 128), F32),
        vm((512, 256), BF), vm((256, 512), BF), vm((16, 256, 256), BF), vm((16, 256, 256), BF),
        vm((16, 128, 128), BF), vm((16, 128, 128), BF),
        vm((4, 4, 128, 128), BF), vm((4, 4, 128, 128), BF),
        vm((4, 128, 2048), BF), vm((4, 128, 2048), BF),
        vm((16, 128, 128), BF), vm((4, 4, 128, 128), BF),
        vm((4, 4, 128, 128), BF),
        vm((4, 4, 128, 128), BF), vm((16, 128, 128), BF),
        vm((512, 512), BF), vm((512, 512), BF),
        vm((4, 4, 128, 128), BF), vm((4, 4, 128, 128), BF),
        vm((4, 128, 2048), BF), vm((2, 128, 2048), BF),
        vm((128, 2048), BF), vm((128, 2048), BF),
        vm((4, 128, 1024), BF), vm((4, 128, 1024), BF),
        vm((4, 128, 1024), BF), vm((4, 4, 32, 1024), BF),
        vm((4, 32, 1024), BF), vm((4, 32, 1024), BF),
        vm((4, 32, 1024), BF), vm((4, 32, 1024), BF),
        vm((32, 2048), BF), vm((32, 2048), BF),
        vm((16, 128, 128), BF), vm((16, 128, 128), BF),
        vm((4, 4, 128, 128), BF), vm((4, 4, 128, 128), BF),
        vm((4, 128, 128), BF), vm((4, 128, 128), BF),
        vm((16, 8, 32, 128), BF), vm((16, 8, 32, 128), BF), vm((16, 8, 32, 256), BF),
        vm((16, 256, 128), F32), vm((16, 256, 128), F32),
        vm((4, 4, 128, 128), BF), vm((4, 32, 2048), BF),
        vm((128, 2048), BF), vm((128, 2048), BF), vm((128, 2048), BF),
        dma((10,)), dma((6,)),
    ]
    for count in (16, 16, 4, 4, 4, 9, 4, 8, 4, 4, 4, 4, 4, 4, 4, 4, 6, 3, 2):
        scratch += [dma((count,)), dma((count,))]
    anywhere = pl.BlockSpec(memory_space=pl.ANY)
    block, query, key, value, filt, weight = pl.pallas_call(
        kernel,
        name="hyena_block",
        out_shape=(
            jax.ShapeDtypeStruct((128, 2048), BF),
            jax.ShapeDtypeStruct((128, 2048), BF),
            jax.ShapeDtypeStruct((128, 2048), BF),
            jax.ShapeDtypeStruct((128, 2048), BF),
            jax.ShapeDtypeStruct((4, 4, 128, 128), BF),
            jax.ShapeDtypeStruct((4, 32, 2048), BF),
        ),
        in_specs=[anywhere] * 10,
        out_specs=[anywhere] * 6,
        scratch_shapes=scratch,
        compiler_params=pltpu.CompilerParams(
            collective_id=0, has_side_effects=True, vmem_limit_bytes=58 << 20
        ),
    )(
        queries[0], key_proj[0], value_proj[0], filters.reshape(16, 128, 128), out_weight,
        out_grad[0], *tables,
    )
    block, query, key, value, filt, weight = pl.pallas_call(
        finish,
        name="finish",
        out_shape=(
            jax.ShapeDtypeStruct((128, 2048), BF),
            jax.ShapeDtypeStruct((128, 2048), BF),
            jax.ShapeDtypeStruct((128, 2048), BF),
            jax.ShapeDtypeStruct((128, 2048), BF),
            jax.ShapeDtypeStruct((2048, 128), F32),
            jax.ShapeDtypeStruct((128, 2048), F32),
        ),
        in_specs=[anywhere] * 6,
        out_specs=[anywhere] * 6,
        scratch_shapes=[
            vm((2048, 128), BF), vm((128, 2048), BF), vm((2048, 128), F32), vm((128, 2048), F32),
            vm((4, 128, 2048), BF), dma((12,)),
        ],
        compiler_params=pltpu.CompilerParams(vmem_limit_bytes=58 << 20),
    )(block, query, key, value, filt.reshape(2048, 128), weight.reshape(128, 2048))
    return block[None], query[None], key[None], value[None], filt, weight


def solution(mesh):
    rows = P("dp", "ctx", None)
    return jax.shard_map(
        shards,
        mesh=mesh,
        in_specs=(rows, rows, rows, P(None, "ctx"), P("ctx", None), rows),
        out_specs=(rows, rows, rows, rows, P(None, "ctx"), P("ctx", None)),
        check_vma=False,
    )
```

```python
import math

import jax
import jax.numpy as jnp
import ml_dtypes
import numpy as np
from jax import lax
from jax.experimental import pallas as pl
from jax.experimental.pallas import tpu as pltpu
from jax.sharding import PartitionSpec as P

MESH = pl.DeviceIdType.MESH
BF = jnp.bfloat16
F32 = jnp.float32

COLS_W = 768


def make_tables():
    k0 = np.arange(16)
    t1 = np.arange(16)
    angle = 2.0 * np.pi * (k0[:, None] + 0.5) * t1[None, :] / 32.0
    outer = np.stack([np.cos(angle), -np.sin(angle)], axis=1)
    outer = np.einsum("krt,su->krstu", outer, np.eye(16)).reshape(512, 256)
    t0 = np.arange(128)
    k1 = np.arange(128)
    angle = (k0[:, None, None] + 0.5) * t0[None, None, :] / 4096.0 + (
        (k1[None, :, None] * t0[None, None, :]) % 128
    ) / 128.0
    cos = np.cos(2.0 * np.pi * angle).reshape(16, 128, 8, 16)
    sin = np.sin(2.0 * np.pi * angle).reshape(16, 128, 8, 16)
    inner = np.empty((16, 2, 128, 8, 2, 16))
    inner[:, 0, :, :, 0] = cos
    inner[:, 0, :, :, 1] = sin
    inner[:, 1, :, :, 0] = -sin
    inner[:, 1, :, :, 1] = cos
    inner = inner.reshape(16, 256, 256)
    return tuple(
        np.ascontiguousarray(table).astype(ml_dtypes.bfloat16)
        for table in (outer, outer.T, inner, inner.transpose(0, 2, 1))
    )


def dot(a, b):
    return jnp.dot(a, b, preferred_element_type=F32)


def times(a, b, conj):
    ar, ai, br, bi = a[:128], a[128:], b[:128], b[128:]
    if conj:
        return jnp.concatenate([ar * br + ai * bi, ar * bi - ai * br], axis=0)
    return jnp.concatenate([ar * br - ai * bi, ar * bi + ai * br], axis=0)


def loop(n, body, unroll=1):
    def step(at, carry):
        body(at)
        return carry

    lax.fori_loop(0, n, step, 0, unroll=unroll)


def rows16(g):
    return pl.ds(pl.multiple_of(g * 16, 16), 16)


def kernel(
    q_in, k_in, v_in, h_in, w_in, g_in, p1_in, p1t_in, m_in, mt_in,
    block_out, query_out, key_out, value_out, filter_out, weight_out,
    q_v, k_v, v_v, h_v, p1, p1t, m_t, mt_t,
    mixed_send, mixed_recv, q_send, q_tile, g_tile, w_tile,
    conv_send, conv_tile, gg_tile, cg_send, cg_recv, gated, gated_t,
    qg_send, qg_recv, block_send, block_core, block_red, block_far,
    wga_send, wga_recv, wgb_send, wgb_recv, wsa_send, wsa_recv, wsb_send, wsb_recv,
    wx_send, wx_recv, mg_send, mg_recv, f_send, f_recv, fx_send, fx_recv,
    s_buf, u_buf, u2_buf, h_spec, m_spec,
    f_total, w_total, block_v, key_v, value_v, lsem, osem,
    mixed_s, mixed_r, mg_s, mg_r, q_s, q_r, w_s, w_r, wq_s, wq_r, wf_s, wf_r, conv_s, conv_r,
    cg_s, cg_r, qg_s, qg_r, wga_s, wga_r, wgb_s, wgb_r, wsa_s, wsa_r, wsb_s, wsb_r, wa_s, wa_r,
    f_s, f_r, fa_s, fa_r, g_s, g_r, block_s, block_r, x_s, x_r,
):
    dp = lax.axis_index("dp")
    me = lax.axis_index("ctx")
    i = lax.div(me, 4)
    j = lax.rem(me, 4)
    far = lax.div(j, 2)
    core = lax.rem(j, 2)
    z = lax.rem(dp, 4)
    j_core = far * 2 + (1 - core)
    j_far = (1 - far) * 2 + core
    near = lax.rem(dp + 4, 8)

    def ctx_peer(at):
        return lax.rem(me + at, 16)

    def z_peer(at):
        return lax.rem(z + at, 4)

    def to_z(at):
        return dp - z + z_peer(at)

    def i_peer(at):
        return lax.rem(i + at, 4)

    def j_peer(at):
        return lax.rem(j + at, 4)

    def remote(src, dst, s, r, to_dp, to_ctx):
        return pltpu.make_async_remote_copy(
            src_ref=src, dst_ref=dst, send_sem=s, recv_sem=r,
            device_id=(to_dp, to_ctx), device_id_type=MESH,
        )

    def mixed_copy(at):
        p = ctx_peer(at)
        return remote(mixed_send.at[p], mixed_recv.at[me], mixed_s.at[at], mixed_r.at[at], dp, p)

    def mg_copy(at):
        p = ctx_peer(at)
        return remote(mg_send.at[p], mg_recv.at[me], mg_s.at[at], mg_r.at[at], dp, p)

    def q_copy(at):
        p = j_peer(at)
        return remote(q_send.at[p], q_tile.at[:, j], q_s.at[at], q_r.at[at], dp, i * 4 + p)

    def g_core(at):
        rows = pl.ds(at * 64, 64)
        return remote(
            g_in.at[rows], g_tile.at[j, rows], g_s.at[at], g_r.at[at], dp, i * 4 + j_core
        )

    def g_far(at):
        rows = pl.ds(at * 64, 64)
        return remote(
            g_in.at[rows], g_tile.at[j, rows], g_s.at[2 + at], g_r.at[2 + at], dp, i * 4 + j_far
        )

    def g_pass(at):
        rows = pl.ds(at * 64, 64)
        ref = g_tile.at[j_far, rows]
        return remote(ref, ref, g_s.at[4 + at], g_r.at[4 + at], dp, i * 4 + j_core)

    def w_copy(at):
        cols = pl.ds(0, COLS_W)
        return remote(
            w_in.at[:, cols], w_tile.at[i, :, cols], w_s.at[at], w_r.at[at],
            dp, i_peer(at) * 4 + j,
        )

    def w_part():
        return pl.ds(pl.multiple_of(z * 32, 32), 32), pl.ds(COLS_W, 2048 - COLS_W)

    def wq_copy(at):
        rows, cols = w_part()
        return remote(
            w_in.at[rows, cols], w_tile.at[i, rows, cols], wq_s.at[at], wq_r.at[at],
            dp, i_peer(at) * 4 + j,
        )

    def wf_copy(at):
        rows, cols = w_part()
        ref = w_tile.at[i_peer(1 + lax.rem(at, 3)), rows, cols]
        return remote(ref, ref, wf_s.at[at], wf_r.at[at], to_z(1 + lax.div(at, 3)), me)

    def conv_copy(at):
        p = i_peer(at)
        return remote(
            conv_send.at[pl.ds(p * 4, 4)], conv_tile.at[i], conv_s.at[at], conv_r.at[at],
            dp, p * 4 + j,
        )

    def cg_half(at, side, first):
        p = i_peer(at)
        return remote(
            cg_send.at[p, pl.ds(side * 2, 2)], cg_recv.at[pl.ds(i * 4 + side * 2, 2)],
            cg_s.at[first + at], cg_r.at[first + at], dp, p * 4 + j,
        )

    def cg_mine(at):
        return cg_half(at, far, 0)

    def cg_other(at):
        return cg_half(at, 1 - far, 4)

    def qg_copy(at):
        p = j_peer(at)
        return remote(qg_send.at[p], qg_recv.at[j], qg_s.at[at], qg_r.at[at], dp, i * 4 + p)

    def block_near(at):
        return remote(
            block_send.at[at * 2 + 1 - core], block_core.at[at], block_s.at[at], block_r.at[at],
            dp, i * 4 + j_core,
        )

    def block_cross(at):
        return remote(block_red, block_far, block_s.at[2], block_r.at[2], dp, i * 4 + j_far)

    def wga_copy(at):
        p = i_peer(at)
        return remote(wga_send.at[p], wga_recv.at[at], wga_s.at[at], wga_r.at[at], dp, p * 4 + j)

    def wgb_copy(at):
        rows = pl.ds(pl.multiple_of(z_peer(at) * 32, 32), 32)
        return remote(
            wgb_send.at[:, rows], wgb_recv.at[at], wgb_s.at[at], wgb_r.at[at], to_z(at), me
        )

    def wsa_copy(at):
        return remote(
            wsa_send.at[z_peer(at)], wsa_recv.at[at], wsa_s.at[at], wsa_r.at[at], to_z(at), me
        )

    def wsb_copy(at):
        p = i_peer(at)
        return remote(wsb_send.at[p], wsb_recv.at[at], wsb_s.at[at], wsb_r.at[at], dp, p * 4 + j)

    def wx_copy(at):
        return remote(wx_send, wx_recv, x_s.at[0], x_r.at[0], near, me)

    def wa_copy(at):
        return remote(w_total.at[z], w_total.at[z], wa_s.at[at], wa_r.at[at], to_z(at), me)

    def f_copy(at):
        return remote(f_send.at[z_peer(at)], f_recv.at[at], f_s.at[at], f_r.at[at], to_z(at), me)

    def fx_copy(at):
        return remote(fx_send, fx_recv, x_s.at[1], x_r.at[1], near, me)

    def fa_copy(at):
        return remote(f_total.at[z], f_total.at[z], fa_s.at[at], fa_r.at[at], to_z(at), me)

    def leave(at, src, dst):
        return pltpu.make_async_copy(src, dst, osem.at[at])

    def each(copy, n, what):
        loop(n - 1, lambda at: getattr(copy(at + 1), what)())

    local = [
        pltpu.make_async_copy(src, dst, lsem.at[at])
        for at, (src, dst) in enumerate(
            [
                (k_in, k_v), (v_in, v_v), (q_in, q_v), (h_in, h_v), (p1_in, p1), (m_in, m_t),
                (mt_in, mt_t), (p1t_in, p1t), (g_in, g_tile.at[j]), (w_in, w_tile.at[i]),
            ]
        )
    ]
    local[0].start()
    local[1].start()

    barrier = pltpu.get_barrier_semaphore()

    def greet_ctx(at):
        pl.semaphore_signal(
            barrier, inc=1, device_id=(dp, ctx_peer(at + 1)), device_id_type=MESH
        )

    def greet_z(at):
        pl.semaphore_signal(barrier, inc=1, device_id=(to_z(at + 1), me), device_id_type=MESH)

    loop(15, greet_ctx)
    loop(3, greet_z)
    pl.semaphore_signal(barrier, inc=1, device_id=(near, me), device_id_type=MESH)

    local[0].wait()
    local[1].wait()
    for at in range(2, 10):
        local[at].start()
    for p in range(16):
        lanes = slice(p * 128, p * 128 + 128)
        mixed_send[p] = (k_v[:, lanes].astype(F32) * v_v[:, lanes].astype(F32)).astype(BF)
    local[2].wait()
    for p in range(16):
        q_send[p % 4, p // 4] = q_v[:, p * 128 : p * 128 + 128]

    pl.semaphore_wait(barrier, 19)
    each(wq_copy, 4, "start")
    each(mixed_copy, 16, "start")
    mixed_recv[me] = mixed_send[me]
    q_tile[:, j] = q_send[j]

    def outer_step(x_ref):
        def body(g):
            x = x_ref[:, rows16(g), :].astype(BF).reshape(256, 128)
            s_buf[:, g] = dot(p1[...], x).reshape(16, 32, 128).astype(BF)

        loop(8, body, 2)

    def inner(k0):
        return dot(m_t[k0], s_buf[k0].reshape(256, 128))

    for at in range(3, 8):
        local[at].wait()
    outer_step(h_v)

    def filter_step(k0):
        h_spec[k0] = inner(k0)

    loop(16, filter_step, 2)

    for at in range(2):
        g_far(at).start()
        g_core(at).start()
    each(w_copy, 4, "start")
    each(q_copy, 4, "start")
    each(wq_copy, 4, "wait_recv")
    loop(9, lambda at: wf_copy(at).start())

    each(mixed_copy, 16, "wait_recv")
    outer_step(mixed_recv)

    def conv_step(k0):
        spec = inner(k0)
        m_spec[k0] = spec
        y = times(h_spec[k0], spec, False).astype(BF)
        u_buf[k0] = dot(mt_t[k0], y).reshape(8, 32, 128).astype(BF)

    loop(16, conv_step, 4)

    def conv_last(g):
        y = dot(p1t[...], u_buf[:, g].reshape(512, 128)) * (1.0 / 2048.0)
        conv_send[:, rows16(g), :] = y.reshape(16, 16, 128).astype(BF)

    loop(8, conv_last, 2)
    each(conv_copy, 4, "start")
    conv_tile[i] = conv_send[pl.ds(i * 4, 4)]

    for at in range(2):
        g_far(at).wait_recv()
        g_pass(at).start()

    local[8].wait()
    local[9].wait()

    def grad_rows(side):
        rows = pl.ds(side * 2, 2)
        for half in range(2):
            wide = lax.dot_general(
                g_tile[rows].reshape(256, 2048),
                w_tile[2 * half : 2 * half + 2].reshape(256, 2048),
                (((1,), (1,)), ((), ())),
                preferred_element_type=F32,
            ).astype(BF)
            for at in range(2):
                part = 2 * half + at
                gg = wide[:, at * 128 : at * 128 + 128].reshape(2, 128, 128)
                gg_tile[part, rows] = gg
                cg_send[part, rows] = (
                    gg.astype(F32) * q_tile[part, rows].astype(F32)
                ).astype(BF)

    each(w_copy, 4, "wait_recv")
    loop(9, lambda at: wf_copy(at).wait_recv())
    for at in range(2):
        g_core(at).wait_recv()
    each(q_copy, 4, "wait_recv")
    grad_rows(far)
    each(cg_mine, 4, "start")
    for at in range(2):
        g_pass(at).wait_recv()
    grad_rows(1 - far)
    each(cg_other, 4, "start")
    cg_recv[pl.ds(i * 4, 4)] = cg_send[i]

    each(conv_copy, 4, "wait_recv")
    for part in range(4):
        conv = conv_tile[part].astype(F32)
        gate = (conv * q_tile[part].astype(F32)).astype(BF).reshape(512, 128)
        gated[:, part * 128 : part * 128 + 128] = gate
        gated_t[part * 128 : part * 128 + 128, :] = gate.astype(F32).T.astype(BF)
        qg = (conv * gg_tile[part].astype(F32)).astype(BF)
        for at in range(4):
            qg_send[at, part] = qg[at]
    each(qg_copy, 4, "start")
    qg_recv[j] = qg_send[j]

    def block_step(n):
        lanes = pl.ds(pl.multiple_of(n * 256, 256), 256)
        y = dot(gated[...], w_tile[:, :, lanes].reshape(512, 256))
        block_send[:, :, lanes] = y.astype(BF).reshape(4, 128, 256)

    loop(8, block_step)
    block_near(1 - far).start()
    block_near(far).start()

    def wg_step(out, n, first):
        lanes = pl.ds(pl.multiple_of(n * 256, 256), 256)
        cols = pl.ds(pl.multiple_of(first + n * 256, 256), 256)
        y = dot(gated_t[...], g_tile[:, :, cols].reshape(512, 256))
        out[:, :, lanes] = y.astype(BF).reshape(4, 128, 256)

    loop(5, lambda n: wg_step(wga_send, n, 0))
    loop(3, lambda n: wg_step(wgb_send, n, 1280))
    each(wgb_copy, 4, "start")

    block_near(1 - far).wait_recv()

    def bred_step(r):
        block_red[rows16(r), :] = (
            block_send[j_far, rows16(r), :].astype(F32)
            + block_core[1 - far, rows16(r), :].astype(F32)
        ).astype(BF)

    loop(8, bred_step)
    block_cross(0).start()

    each(cg_mine, 4, "wait_recv")
    each(cg_other, 4, "wait_recv")
    each(wga_copy, 4, "start")
    outer_step(cg_recv)

    def back_step(k0):
        spec = inner(k0)
        y = jnp.concatenate(
            [times(h_spec[k0], spec, True), times(m_spec[k0], spec, True)], axis=1
        ).astype(BF)
        u2_buf[k0] = dot(mt_t[k0], y).reshape(8, 32, 256).astype(BF)

    loop(16, back_step, 4)

    def back_last(g):
        y = dot(p1t[...], u2_buf[:, g].reshape(512, 256)) * (1.0 / 2048.0)
        y = y.reshape(16, 16, 256).astype(BF)
        mg_send[:, rows16(g), :] = y[:, :, :128]
        f_send[:, :, rows16(g), :] = y[:, :, 128:].reshape(4, 4, 16, 128)

    loop(8, back_last, 2)
    each(f_copy, 4, "start")
    each(mg_copy, 16, "start")
    mg_recv[me] = mg_send[me]

    each(qg_copy, 4, "wait_recv")
    for p in range(16):
        q_v[:, p * 128 : p * 128 + 128] = qg_recv[p % 4, p // 4]
    leave(0, q_v, query_out).start()

    each(f_copy, 4, "wait_recv")
    total = f_send[z].astype(F32)
    for at in range(1, 4):
        total += f_recv[at].astype(F32)
    fx_send[...] = total.astype(BF)
    fx_copy(0).start()

    each(wga_copy, 4, "wait_recv")

    def suma_step(r):
        total = wga_send[i, rows16(r), :].astype(F32)
        for at in range(1, 4):
            total += wga_recv[at, rows16(r), :].astype(F32)
        wsa_send[lax.div(r, 2), rows16(lax.rem(r, 2)), :] = total.astype(BF)

    loop(8, suma_step)
    each(wsa_copy, 4, "start")
    each(wgb_copy, 4, "wait_recv")

    def sumb_step(r):
        total = wgb_send[r, pl.ds(pl.multiple_of(z * 32, 32), 32), :].astype(F32)
        for at in range(1, 4):
            total += wgb_recv[at, r].astype(F32)
        wsb_send[r] = total.astype(BF)

    loop(4, sumb_step)
    each(wsb_copy, 4, "start")

    fx_copy(0).wait_recv()
    f_total[z] = (fx_send[...].astype(F32) + fx_recv[...].astype(F32)).astype(BF)
    each(fa_copy, 4, "start")

    each(wsa_copy, 4, "wait_recv")
    total = wsa_send[z].astype(F32)
    for at in range(1, 4):
        total += wsa_recv[at].astype(F32)
    wx_send[:, :1280] = total.astype(BF)
    each(wsb_copy, 4, "wait_recv")
    total = wsb_send[i].astype(F32)
    for at in range(1, 4):
        total += wsb_recv[at].astype(F32)
    wx_send[:, 1280:] = total.astype(BF)
    wx_copy(0).start()

    block_near(far).wait_recv()
    block_cross(0).wait_recv()

    def bsum_step(r):
        block_v[rows16(r), :] = (
            block_send[j, rows16(r), :].astype(F32)
            + block_core[far, rows16(r), :].astype(F32)
            + block_far[rows16(r), :].astype(F32)
        ).astype(BF)

    loop(8, bsum_step)
    leave(1, block_v, block_out).start()

    wx_copy(0).wait_recv()
    w_total[z] = (wx_send[...].astype(F32) + wx_recv[...].astype(F32)).astype(BF)
    each(wa_copy, 4, "start")

    each(mg_copy, 16, "wait_recv")
    for p in range(16):
        lanes = slice(p * 128, p * 128 + 128)
        mg = mg_recv[p].astype(F32)
        key_v[:, lanes] = (mg * v_v[:, lanes].astype(F32)).astype(BF)
        value_v[:, lanes] = (mg * k_v[:, lanes].astype(F32)).astype(BF)
    leave(2, key_v, key_out).start()
    leave(5, value_v, value_out).start()

    each(fa_copy, 4, "wait_recv")
    leave(3, f_total, filter_out).start()
    each(wa_copy, 4, "wait_recv")
    leave(4, w_total, weight_out).start()
    each(mixed_copy, 16, "wait_send")
    each(mg_copy, 16, "wait_send")
    for copy in (
        q_copy, w_copy, wq_copy, conv_copy, cg_mine, cg_other, qg_copy, wga_copy, wgb_copy, wsa_copy,
        wsb_copy, wa_copy, f_copy, fa_copy,
    ):
        each(copy, 4, "wait_send")
    loop(9, lambda at: wf_copy(at).wait_send())
    for at in range(2):
        for copy in (g_core, g_far, g_pass, block_near):
            copy(at).wait_send()
    for copy in (block_cross, wx_copy, fx_copy):
        copy(0).wait_send()
    for at, (src, dst) in enumerate(
        [(q_v, query_out), (block_v, block_out), (key_v, key_out), (f_total, filter_out),
         (w_total, weight_out), (value_v, value_out)]
    ):
        leave(at, src, dst).wait()


def finish(
    block_in, query_in, key_in, value_in, filter_in, weight_in,
    block_out, query_out, key_out, value_out, filter_out, weight_out,
    f_v, w_v, f_wide, w_wide, rows, sem,
):
    scale = 1.0 / math.sqrt(16384.0)

    def move(at, src, dst):
        copy = pltpu.make_async_copy(src, dst, sem.at[at])
        copy.start()
        return copy

    loads = [
        move(at, src, dst)
        for at, (src, dst) in enumerate(
            [
                (filter_in, f_v), (weight_in, w_v), (block_in, rows.at[0]),
                (query_in, rows.at[1]), (key_in, rows.at[2]), (value_in, rows.at[3]),
            ]
        )
    ]
    loads[0].wait()
    f_wide[...] = f_v[...].astype(F32) * scale
    moves = [move(6, f_wide, filter_out)]
    loads[1].wait()
    w_wide[...] = w_v[...].astype(F32) * scale
    moves.append(move(7, w_wide, weight_out))
    for at, out in enumerate((block_out, query_out, key_out, value_out)):
        loads[2 + at].wait()
        moves.append(move(8 + at, rows.at[at], out))
    for copy in moves:
        copy.wait()


def shards(queries, key_proj, value_proj, filters, out_weight, out_grad):
    tables = make_tables()
    vm = pltpu.VMEM
    dma = pltpu.SemaphoreType.DMA
    scratch = [
        vm((128, 2048), BF), vm((128, 2048), BF), vm((128, 2048), BF), vm((16, 128, 128), F32),
        vm((512, 256), BF), vm((256, 512), BF), vm((16, 256, 256), BF), vm((16, 256, 256), BF),
        vm((16, 128, 128), BF), vm((16, 128, 128), BF),
        vm((4, 4, 128, 128), BF), vm((4, 4, 128, 128), BF),
        vm((4, 128, 2048), BF), vm((4, 128, 2048), BF),
        vm((16, 128, 128), BF), vm((4, 4, 128, 128), BF),
        vm((4, 4, 128, 128), BF),
        vm((4, 4, 128, 128), BF), vm((16, 128, 128), BF),
        vm((512, 512), BF), vm((512, 512), BF),
        vm((4, 4, 128, 128), BF), vm((4, 4, 128, 128), BF),
        vm((4, 128, 2048), BF), vm((2, 128, 2048), BF),
        vm((128, 2048), BF), vm((128, 2048), BF),
        vm((4, 128, 1280), BF), vm((4, 128, 1280), BF),
        vm((4, 128, 768), BF), vm((4, 4, 32, 768), BF),
        vm((4, 32, 1280), BF), vm((4, 32, 1280), BF),
        vm((4, 32, 768), BF), vm((4, 32, 768), BF),
        vm((32, 2048), BF), vm((32, 2048), BF),
        vm((16, 128, 128), BF), vm((16, 128, 128), BF),
        vm((4, 4, 128, 128), BF), vm((4, 4, 128, 128), BF),
        vm((4, 128, 128), BF), vm((4, 128, 128), BF),
        vm((16, 8, 32, 128), BF), vm((16, 8, 32, 128), BF), vm((16, 8, 32, 256), BF),
        vm((16, 256, 128), F32), vm((16, 256, 128), F32),
        vm((4, 4, 128, 128), BF), vm((4, 32, 2048), BF),
        vm((128, 2048), BF), vm((128, 2048), BF), vm((128, 2048), BF),
        dma((10,)), dma((6,)),
    ]
    for count in (16, 16, 4, 4, 4, 9, 4, 8, 4, 4, 4, 4, 4, 4, 4, 4, 6, 3, 2):
        scratch += [dma((count,)), dma((count,))]
    anywhere = pl.BlockSpec(memory_space=pl.ANY)
    block, query, key, value, filt, weight = pl.pallas_call(
        kernel,
        name="hyena_block",
        out_shape=(
            jax.ShapeDtypeStruct((128, 2048), BF),
            jax.ShapeDtypeStruct((128, 2048), BF),
            jax.ShapeDtypeStruct((128, 2048), BF),
            jax.ShapeDtypeStruct((128, 2048), BF),
            jax.ShapeDtypeStruct((4, 4, 128, 128), BF),
            jax.ShapeDtypeStruct((4, 32, 2048), BF),
        ),
        in_specs=[anywhere] * 10,
        out_specs=[anywhere] * 6,
        scratch_shapes=scratch,
        compiler_params=pltpu.CompilerParams(
            collective_id=0, has_side_effects=True, vmem_limit_bytes=58 << 20
        ),
    )(
        queries[0], key_proj[0], value_proj[0], filters.reshape(16, 128, 128), out_weight,
        out_grad[0], *tables,
    )
    block, query, key, value, filt, weight = pl.pallas_call(
        finish,
        name="finish",
        out_shape=(
            jax.ShapeDtypeStruct((128, 2048), BF),
            jax.ShapeDtypeStruct((128, 2048), BF),
            jax.ShapeDtypeStruct((128, 2048), BF),
            jax.ShapeDtypeStruct((128, 2048), BF),
            jax.ShapeDtypeStruct((2048, 128), F32),
            jax.ShapeDtypeStruct((128, 2048), F32),
        ),
        in_specs=[anywhere] * 6,
        out_specs=[anywhere] * 6,
        scratch_shapes=[
            vm((2048, 128), BF), vm((128, 2048), BF), vm((2048, 128), F32), vm((128, 2048), F32),
            vm((4, 128, 2048), BF), dma((12,)),
        ],
        compiler_params=pltpu.CompilerParams(vmem_limit_bytes=58 << 20),
    )(block, query, key, value, filt.reshape(2048, 128), weight.reshape(128, 2048))
    return block[None], query[None], key[None], value[None], filt, weight


def solution(mesh):
    rows = P("dp", "ctx", None)
    return jax.shard_map(
        shards,
        mesh=mesh,
        in_specs=(rows, rows, rows, P(None, "ctx"), P("ctx", None), rows),
        out_specs=(rows, rows, rows, rows, P(None, "ctx"), P("ctx", None)),
        check_vma=False,
    )
```

```python
import math

import jax
import jax.numpy as jnp
import ml_dtypes
import numpy as np
from jax import lax
from jax.experimental import pallas as pl
from jax.experimental.pallas import tpu as pltpu
from jax.sharding import PartitionSpec as P

MESH = pl.DeviceIdType.MESH
BF = jnp.bfloat16
F32 = jnp.float32

COLS_W = 768


def make_tables():
    k0 = np.arange(16)
    t1 = np.arange(16)
    angle = 2.0 * np.pi * (k0[:, None] + 0.5) * t1[None, :] / 32.0
    outer = np.stack([np.cos(angle), -np.sin(angle)], axis=1)
    outer = np.einsum("krt,su->krstu", outer, np.eye(16)).reshape(512, 256)
    t0 = np.arange(128)
    k1 = np.arange(128)
    angle = (k0[:, None, None] + 0.5) * t0[None, None, :] / 4096.0 + (
        (k1[None, :, None] * t0[None, None, :]) % 128
    ) / 128.0
    cos = np.cos(2.0 * np.pi * angle).reshape(16, 128, 8, 16)
    sin = np.sin(2.0 * np.pi * angle).reshape(16, 128, 8, 16)
    inner = np.empty((16, 2, 128, 8, 2, 16))
    inner[:, 0, :, :, 0] = cos
    inner[:, 0, :, :, 1] = sin
    inner[:, 1, :, :, 0] = -sin
    inner[:, 1, :, :, 1] = cos
    inner = inner.reshape(16, 256, 256)
    return tuple(
        np.ascontiguousarray(table).astype(ml_dtypes.bfloat16)
        for table in (outer, outer.T, inner, inner.transpose(0, 2, 1))
    )


def dot(a, b):
    return jnp.dot(a, b, preferred_element_type=F32)


def times(a, b, conj):
    ar, ai, br, bi = a[:128], a[128:], b[:128], b[128:]
    if conj:
        return jnp.concatenate([ar * br + ai * bi, ar * bi - ai * br], axis=0)
    return jnp.concatenate([ar * br - ai * bi, ar * bi + ai * br], axis=0)


def loop(n, body, unroll=1):
    def step(at, carry):
        body(at)
        return carry

    lax.fori_loop(0, n, step, 0, unroll=unroll)


def rows16(g):
    return pl.ds(pl.multiple_of(g * 16, 16), 16)


def kernel(
    q_in, k_in, v_in, h_in, w_in, g_in, p1_in, p1t_in, m_in, mt_in,
    block_out, query_out, key_out, value_out, filter_out, weight_out,
    q_v, k_v, v_v, h_v, p1, p1t, m_t, mt_t,
    mixed_send, mixed_recv, q_send, q_tile, g_tile, w_tile,
    conv_send, conv_tile, gg_tile, cg_send, cg_recv, gated, gated_t,
    qg_send, qg_recv, block_send, block_core, block_red, block_far,
    wga_send, wga_recv, wgb_send, wgb_recv, wsa_send, wsa_recv, wsb_send, wsb_recv,
    wx_send, wx_recv, mg_send, mg_recv, f_send, f_recv, fx_send, fx_recv,
    s_buf, u_buf, u2_buf, h_spec, m_spec,
    f_total, w_total, block_v, key_v, value_v, lsem, osem,
    mixed_s, mixed_r, mg_s, mg_r, q_s, q_r, w_s, w_r, wq_s, wq_r, wf_s, wf_r, conv_s, conv_r,
    cg_s, cg_r, qg_s, qg_r, wga_s, wga_r, wgb_s, wgb_r, wsa_s, wsa_r, wsb_s, wsb_r, wa_s, wa_r,
    f_s, f_r, fa_s, fa_r, g_s, g_r, block_s, block_r, x_s, x_r,
):
    dp = lax.axis_index("dp")
    me = lax.axis_index("ctx")
    i = lax.div(me, 4)
    j = lax.rem(me, 4)
    far = lax.div(j, 2)
    core = lax.rem(j, 2)
    z = lax.rem(dp, 4)
    j_core = far * 2 + (1 - core)
    j_far = (1 - far) * 2 + core
    near = lax.rem(dp + 4, 8)

    def ctx_peer(at):
        return lax.rem(me + at, 16)

    def z_peer(at):
        return lax.rem(z + at, 4)

    def to_z(at):
        return dp - z + z_peer(at)

    def i_peer(at):
        return lax.rem(i + at, 4)

    def j_peer(at):
        return lax.rem(j + at, 4)

    def remote(src, dst, s, r, to_dp, to_ctx):
        return pltpu.make_async_remote_copy(
            src_ref=src, dst_ref=dst, send_sem=s, recv_sem=r,
            device_id=(to_dp, to_ctx), device_id_type=MESH,
        )

    def mixed_copy(at):
        p = ctx_peer(at)
        return remote(mixed_send.at[p], mixed_recv.at[me], mixed_s.at[at], mixed_r.at[at], dp, p)

    def mg_copy(at):
        p = ctx_peer(at)
        return remote(mg_send.at[p], mg_recv.at[me], mg_s.at[at], mg_r.at[at], dp, p)

    def q_copy(at):
        p = j_peer(at)
        return remote(q_send.at[p], q_tile.at[:, j], q_s.at[at], q_r.at[at], dp, i * 4 + p)

    def g_core(at):
        rows = pl.ds(at * 64, 64)
        return remote(
            g_in.at[rows], g_tile.at[j, rows], g_s.at[at], g_r.at[at], dp, i * 4 + j_core
        )

    def g_far(at):
        rows = pl.ds(at * 64, 64)
        return remote(
            g_in.at[rows], g_tile.at[j, rows], g_s.at[2 + at], g_r.at[2 + at], dp, i * 4 + j_far
        )

    def g_pass(at):
        rows = pl.ds(at * 64, 64)
        ref = g_tile.at[j_far, rows]
        return remote(ref, ref, g_s.at[4 + at], g_r.at[4 + at], dp, i * 4 + j_core)

    def w_copy(at):
        cols = pl.ds(0, COLS_W)
        return remote(
            w_in.at[:, cols], w_tile.at[i, :, cols], w_s.at[at], w_r.at[at],
            dp, i_peer(at) * 4 + j,
        )

    def w_part():
        return pl.ds(pl.multiple_of(z * 32, 32), 32), pl.ds(COLS_W, 2048 - COLS_W)

    def wq_copy(at):
        rows, cols = w_part()
        return remote(
            w_in.at[rows, cols], w_tile.at[i, rows, cols], wq_s.at[at], wq_r.at[at],
            dp, i_peer(at) * 4 + j,
        )

    def wf_copy(at):
        rows, cols = w_part()
        ref = w_tile.at[i_peer(1 + lax.rem(at, 3)), rows, cols]
        return remote(ref, ref, wf_s.at[at], wf_r.at[at], to_z(1 + lax.div(at, 3)), me)

    def conv_copy(at):
        p = i_peer(at)
        return remote(
            conv_send.at[pl.ds(p * 4, 4)], conv_tile.at[i], conv_s.at[at], conv_r.at[at],
            dp, p * 4 + j,
        )

    def cg_half(at, side, first):
        p = i_peer(at)
        return remote(
            cg_send.at[p, pl.ds(side * 2, 2)], cg_recv.at[pl.ds(i * 4 + side * 2, 2)],
            cg_s.at[first + at], cg_r.at[first + at], dp, p * 4 + j,
        )

    def cg_mine(at):
        return cg_half(at, far, 0)

    def cg_other(at):
        return cg_half(at, 1 - far, 4)

    def qg_copy(at):
        p = j_peer(at)
        return remote(qg_send.at[p], qg_recv.at[j], qg_s.at[at], qg_r.at[at], dp, i * 4 + p)

    def block_near(at):
        return remote(
            block_send.at[at * 2 + 1 - core], block_core.at[at], block_s.at[at], block_r.at[at],
            dp, i * 4 + j_core,
        )

    def block_cross(at):
        return remote(block_red, block_far, block_s.at[2], block_r.at[2], dp, i * 4 + j_far)

    def wga_copy(at):
        p = i_peer(at)
        return remote(wga_send.at[p], wga_recv.at[at], wga_s.at[at], wga_r.at[at], dp, p * 4 + j)

    def wgb_copy(at):
        rows = pl.ds(pl.multiple_of(z_peer(at) * 32, 32), 32)
        return remote(
            wgb_send.at[:, rows], wgb_recv.at[at], wgb_s.at[at], wgb_r.at[at], to_z(at), me
        )

    def wsa_copy(at):
        return remote(
            wsa_send.at[z_peer(at)], wsa_recv.at[at], wsa_s.at[at], wsa_r.at[at], to_z(at), me
        )

    def wsb_copy(at):
        p = i_peer(at)
        return remote(wsb_send.at[p], wsb_recv.at[at], wsb_s.at[at], wsb_r.at[at], dp, p * 4 + j)

    def wx_copy(at):
        return remote(wx_send, wx_recv, x_s.at[0], x_r.at[0], near, me)

    def wa_copy(at):
        return remote(w_total.at[z], w_total.at[z], wa_s.at[at], wa_r.at[at], to_z(at), me)

    def f_copy(at):
        return remote(f_send.at[z_peer(at)], f_recv.at[at], f_s.at[at], f_r.at[at], to_z(at), me)

    def fx_copy(at):
        return remote(fx_send, fx_recv, x_s.at[1], x_r.at[1], near, me)

    def fa_copy(at):
        return remote(f_total.at[z], f_total.at[z], fa_s.at[at], fa_r.at[at], to_z(at), me)

    def leave(at, src, dst):
        return pltpu.make_async_copy(src, dst, osem.at[at])

    def each(copy, n, what):
        loop(n - 1, lambda at: getattr(copy(at + 1), what)())

    local = [
        pltpu.make_async_copy(src, dst, lsem.at[at])
        for at, (src, dst) in enumerate(
            [
                (k_in, k_v), (v_in, v_v), (q_in, q_v), (h_in, h_v), (p1_in, p1), (m_in, m_t),
                (mt_in, mt_t), (p1t_in, p1t), (g_in, g_tile.at[j]), (w_in, w_tile.at[i]),
            ]
        )
    ]
    local[0].start()
    local[1].start()

    barrier = pltpu.get_barrier_semaphore()

    def greet_ctx(at):
        pl.semaphore_signal(
            barrier, inc=1, device_id=(dp, ctx_peer(at + 1)), device_id_type=MESH
        )

    def greet_z(at):
        pl.semaphore_signal(barrier, inc=1, device_id=(to_z(at + 1), me), device_id_type=MESH)

    loop(15, greet_ctx)
    loop(3, greet_z)
    pl.semaphore_signal(barrier, inc=1, device_id=(near, me), device_id_type=MESH)

    local[0].wait()
    local[1].wait()
    for at in range(2, 10):
        local[at].start()
    for p in range(16):
        lanes = slice(p * 128, p * 128 + 128)
        mixed_send[p] = (k_v[:, lanes].astype(F32) * v_v[:, lanes].astype(F32)).astype(BF)
    local[2].wait()
    for p in range(16):
        q_send[p % 4, p // 4] = q_v[:, p * 128 : p * 128 + 128]

    pl.semaphore_wait(barrier, 19)
    each(wq_copy, 4, "start")
    each(mixed_copy, 16, "start")
    mixed_recv[me] = mixed_send[me]
    q_tile[:, j] = q_send[j]

    def outer_step(x_ref):
        def body(g):
            x = x_ref[:, rows16(g), :].astype(BF).reshape(256, 128)
            s_buf[:, g] = dot(p1[...], x).reshape(16, 32, 128).astype(BF)

        loop(8, body, 2)

    def inner(k0):
        return dot(m_t[k0], s_buf[k0].reshape(256, 128))

    for at in range(3, 8):
        local[at].wait()
    outer_step(h_v)

    def filter_step(k0):
        h_spec[k0] = inner(k0)

    loop(16, filter_step, 2)

    for at in range(2):
        g_far(at).start()
        g_core(at).start()
    each(w_copy, 4, "start")
    each(q_copy, 4, "start")
    each(wq_copy, 4, "wait_recv")
    loop(9, lambda at: wf_copy(at).start())

    each(mixed_copy, 16, "wait_recv")
    outer_step(mixed_recv)

    def conv_step(k0):
        spec = inner(k0)
        m_spec[k0] = spec
        y = times(h_spec[k0], spec, False).astype(BF)
        u_buf[k0] = dot(mt_t[k0], y).reshape(8, 32, 128).astype(BF)

    loop(16, conv_step, 4)

    def conv_last(g):
        y = dot(p1t[...], u_buf[:, g].reshape(512, 128)) * (1.0 / 2048.0)
        conv_send[:, rows16(g), :] = y.reshape(16, 16, 128).astype(BF)

    loop(8, conv_last, 2)
    each(conv_copy, 4, "start")
    conv_tile[i] = conv_send[pl.ds(i * 4, 4)]

    for at in range(2):
        g_far(at).wait_recv()
        g_pass(at).start()

    local[8].wait()
    local[9].wait()

    def grad_rows(side):
        rows = pl.ds(side * 2, 2)
        for half in range(2):
            wide = lax.dot_general(
                g_tile[rows].reshape(256, 2048),
                w_tile[2 * half : 2 * half + 2].reshape(256, 2048),
                (((1,), (1,)), ((), ())),
                preferred_element_type=F32,
            ).astype(BF)
            for at in range(2):
                part = 2 * half + at
                gg = wide[:, at * 128 : at * 128 + 128].reshape(2, 128, 128)
                gg_tile[part, rows] = gg
                cg_send[part, rows] = (
                    gg.astype(F32) * q_tile[part, rows].astype(F32)
                ).astype(BF)

    each(w_copy, 4, "wait_recv")
    loop(9, lambda at: wf_copy(at).wait_recv())
    for at in range(2):
        g_core(at).wait_recv()
    each(q_copy, 4, "wait_recv")
    grad_rows(far)
    each(cg_mine, 4, "start")
    for at in range(2):
        g_pass(at).wait_recv()
    grad_rows(1 - far)
    each(cg_other, 4, "start")
    cg_recv[pl.ds(i * 4, 4)] = cg_send[i]

    each(conv_copy, 4, "wait_recv")
    for part in range(4):
        conv = conv_tile[part].astype(F32)
        gate = (conv * q_tile[part].astype(F32)).astype(BF).reshape(512, 128)
        gated[:, part * 128 : part * 128 + 128] = gate
        gated_t[part * 128 : part * 128 + 128, :] = gate.astype(F32).T.astype(BF)
        qg = (conv * gg_tile[part].astype(F32)).astype(BF)
        for at in range(4):
            qg_send[at, part] = qg[at]
    each(qg_copy, 4, "start")
    qg_recv[j] = qg_send[j]

    def block_step(n):
        lanes = pl.ds(pl.multiple_of(n * 256, 256), 256)
        y = dot(gated[...], w_tile[:, :, lanes].reshape(512, 256))
        block_send[:, :, lanes] = y.astype(BF).reshape(4, 128, 256)

    loop(8, block_step)
    block_near(1 - far).start()
    block_near(far).start()

    def wg_step(out, n, first):
        lanes = pl.ds(pl.multiple_of(n * 256, 256), 256)
        cols = pl.ds(pl.multiple_of(first + n * 256, 256), 256)
        y = dot(gated_t[...], g_tile[:, :, cols].reshape(512, 256))
        out[:, :, lanes] = y.astype(BF).reshape(4, 128, 256)

    loop(5, lambda n: wg_step(wga_send, n, 0))
    loop(3, lambda n: wg_step(wgb_send, n, 1280))
    each(wgb_copy, 4, "start")

    block_near(1 - far).wait_recv()

    def bred_step(r):
        block_red[rows16(r), :] = (
            block_send[j_far, rows16(r), :].astype(F32)
            + block_core[1 - far, rows16(r), :].astype(F32)
        ).astype(BF)

    loop(8, bred_step)
    block_cross(0).start()

    each(cg_mine, 4, "wait_recv")
    each(cg_other, 4, "wait_recv")
    each(wga_copy, 4, "start")
    outer_step(cg_recv)

    def back_step(k0):
        spec = inner(k0)
        y = jnp.concatenate(
            [times(h_spec[k0], spec, True), times(m_spec[k0], spec, True)], axis=1
        ).astype(BF)
        u2_buf[k0] = dot(mt_t[k0], y).reshape(8, 32, 256).astype(BF)

    loop(16, back_step, 4)

    def back_last(g):
        y = dot(p1t[...], u2_buf[:, g].reshape(512, 256)) * (1.0 / 2048.0)
        y = y.reshape(16, 16, 256).astype(BF)
        mg_send[:, rows16(g), :] = y[:, :, :128]
        f_send[:, :, rows16(g), :] = y[:, :, 128:].reshape(4, 4, 16, 128)

    loop(8, back_last, 2)
    each(f_copy, 4, "start")
    each(mg_copy, 16, "start")
    mg_recv[me] = mg_send[me]

    each(qg_copy, 4, "wait_recv")
    for p in range(16):
        q_v[:, p * 128 : p * 128 + 128] = qg_recv[p % 4, p // 4]
    leave(0, q_v, query_out).start()

    each(f_copy, 4, "wait_recv")
    total = f_send[z].astype(F32)
    for at in range(1, 4):
        total += f_recv[at].astype(F32)
    fx_send[...] = total.astype(BF)
    fx_copy(0).start()

    each(wga_copy, 4, "wait_recv")

    def suma_step(r):
        total = wga_send[i, rows16(r), :].astype(F32)
        for at in range(1, 4):
            total += wga_recv[at, rows16(r), :].astype(F32)
        wsa_send[lax.div(r, 2), rows16(lax.rem(r, 2)), :] = total.astype(BF)

    loop(8, suma_step)
    each(wsa_copy, 4, "start")
    each(wgb_copy, 4, "wait_recv")

    def sumb_step(r):
        total = wgb_send[r, pl.ds(pl.multiple_of(z * 32, 32), 32), :].astype(F32)
        for at in range(1, 4):
            total += wgb_recv[at, r].astype(F32)
        wsb_send[r] = total.astype(BF)

    loop(4, sumb_step)
    each(wsb_copy, 4, "start")

    fx_copy(0).wait_recv()
    f_total[z] = (fx_send[...].astype(F32) + fx_recv[...].astype(F32)).astype(BF)
    each(fa_copy, 4, "start")

    each(wsa_copy, 4, "wait_recv")
    total = wsa_send[z].astype(F32)
    for at in range(1, 4):
        total += wsa_recv[at].astype(F32)
    wx_send[:, :1280] = total.astype(BF)
    each(wsb_copy, 4, "wait_recv")
    total = wsb_send[i].astype(F32)
    for at in range(1, 4):
        total += wsb_recv[at].astype(F32)
    wx_send[:, 1280:] = total.astype(BF)
    wx_copy(0).start()

    block_near(far).wait_recv()
    block_cross(0).wait_recv()

    def bsum_step(r):
        block_v[rows16(r), :] = (
            block_send[j, rows16(r), :].astype(F32)
            + block_core[far, rows16(r), :].astype(F32)
            + block_far[rows16(r), :].astype(F32)
        ).astype(BF)

    loop(8, bsum_step)
    leave(1, block_v, block_out).start()

    wx_copy(0).wait_recv()
    w_total[z] = (wx_send[...].astype(F32) + wx_recv[...].astype(F32)).astype(BF)
    each(wa_copy, 4, "start")

    each(mg_copy, 16, "wait_recv")
    for p in range(16):
        lanes = slice(p * 128, p * 128 + 128)
        mg = mg_recv[p].astype(F32)
        key_v[:, lanes] = (mg * v_v[:, lanes].astype(F32)).astype(BF)
        value_v[:, lanes] = (mg * k_v[:, lanes].astype(F32)).astype(BF)
    leave(2, key_v, key_out).start()
    leave(5, value_v, value_out).start()

    each(mixed_copy, 16, "wait_send")
    each(mg_copy, 16, "wait_send")
    for copy in (
        q_copy, w_copy, wq_copy, conv_copy, cg_mine, cg_other, qg_copy, wga_copy, wgb_copy, wsa_copy,
        wsb_copy, f_copy,
    ):
        each(copy, 4, "wait_send")
    loop(9, lambda at: wf_copy(at).wait_send())
    for at in range(2):
        for copy in (g_core, g_far, g_pass, block_near):
            copy(at).wait_send()
    for copy in (block_cross, wx_copy, fx_copy):
        copy(0).wait_send()
    each(fa_copy, 4, "wait_recv")
    leave(3, f_total, filter_out).start()
    each(wa_copy, 4, "wait_recv")
    leave(4, w_total, weight_out).start()
    each(fa_copy, 4, "wait_send")
    each(wa_copy, 4, "wait_send")
    for at, (src, dst) in enumerate(
        [(q_v, query_out), (block_v, block_out), (key_v, key_out), (f_total, filter_out),
         (w_total, weight_out), (value_v, value_out)]
    ):
        leave(at, src, dst).wait()


def finish(
    block_in, query_in, key_in, value_in, filter_in, weight_in,
    block_out, query_out, key_out, value_out, filter_out, weight_out,
    f_v, w_v, f_wide, w_wide, rows, sem,
):
    scale = 1.0 / math.sqrt(16384.0)

    def move(at, src, dst):
        copy = pltpu.make_async_copy(src, dst, sem.at[at])
        copy.start()
        return copy

    loads = [
        move(at, src, dst)
        for at, (src, dst) in enumerate(
            [
                (filter_in, f_v), (weight_in, w_v), (block_in, rows.at[0]),
                (query_in, rows.at[1]), (key_in, rows.at[2]), (value_in, rows.at[3]),
            ]
        )
    ]
    loads[0].wait()
    f_wide[...] = f_v[...].astype(F32) * scale
    moves = [move(6, f_wide, filter_out)]
    loads[1].wait()
    w_wide[...] = w_v[...].astype(F32) * scale
    moves.append(move(7, w_wide, weight_out))
    for at, out in enumerate((block_out, query_out, key_out, value_out)):
        loads[2 + at].wait()
        moves.append(move(8 + at, rows.at[at], out))
    for copy in moves:
        copy.wait()


def shards(queries, key_proj, value_proj, filters, out_weight, out_grad):
    tables = make_tables()
    vm = pltpu.VMEM
    dma = pltpu.SemaphoreType.DMA
    scratch = [
        vm((128, 2048), BF), vm((128, 2048), BF), vm((128, 2048), BF), vm((16, 128, 128), F32),
        vm((512, 256), BF), vm((256, 512), BF), vm((16, 256, 256), BF), vm((16, 256, 256), BF),
        vm((16, 128, 128), BF), vm((16, 128, 128), BF),
        vm((4, 4, 128, 128), BF), vm((4, 4, 128, 128), BF),
        vm((4, 128, 2048), BF), vm((4, 128, 2048), BF),
        vm((16, 128, 128), BF), vm((4, 4, 128, 128), BF),
        vm((4, 4, 128, 128), BF),
        vm((4, 4, 128, 128), BF), vm((16, 128, 128), BF),
        vm((512, 512), BF), vm((512, 512), BF),
        vm((4, 4, 128, 128), BF), vm((4, 4, 128, 128), BF),
        vm((4, 128, 2048), BF), vm((2, 128, 2048), BF),
        vm((128, 2048), BF), vm((128, 2048), BF),
        vm((4, 128, 1280), BF), vm((4, 128, 1280), BF),
        vm((4, 128, 768), BF), vm((4, 4, 32, 768), BF),
        vm((4, 32, 1280), BF), vm((4, 32, 1280), BF),
        vm((4, 32, 768), BF), vm((4, 32, 768), BF),
        vm((32, 2048), BF), vm((32, 2048), BF),
        vm((16, 128, 128), BF), vm((16, 128, 128), BF),
        vm((4, 4, 128, 128), BF), vm((4, 4, 128, 128), BF),
        vm((4, 128, 128), BF), vm((4, 128, 128), BF),
        vm((16, 8, 32, 128), BF), vm((16, 8, 32, 128), BF), vm((16, 8, 32, 256), BF),
        vm((16, 256, 128), F32), vm((16, 256, 128), F32),
        vm((4, 4, 128, 128), BF), vm((4, 32, 2048), BF),
        vm((128, 2048), BF), vm((128, 2048), BF), vm((128, 2048), BF),
        dma((10,)), dma((6,)),
    ]
    for count in (16, 16, 4, 4, 4, 9, 4, 8, 4, 4, 4, 4, 4, 4, 4, 4, 6, 3, 2):
        scratch += [dma((count,)), dma((count,))]
    anywhere = pl.BlockSpec(memory_space=pl.ANY)
    block, query, key, value, filt, weight = pl.pallas_call(
        kernel,
        name="hyena_block",
        out_shape=(
            jax.ShapeDtypeStruct((128, 2048), BF),
            jax.ShapeDtypeStruct((128, 2048), BF),
            jax.ShapeDtypeStruct((128, 2048), BF),
            jax.ShapeDtypeStruct((128, 2048), BF),
            jax.ShapeDtypeStruct((4, 4, 128, 128), BF),
            jax.ShapeDtypeStruct((4, 32, 2048), BF),
        ),
        in_specs=[anywhere] * 10,
        out_specs=[anywhere] * 6,
        scratch_shapes=scratch,
        compiler_params=pltpu.CompilerParams(
            collective_id=0, has_side_effects=True, vmem_limit_bytes=58 << 20
        ),
    )(
        queries[0], key_proj[0], value_proj[0], filters.reshape(16, 128, 128), out_weight,
        out_grad[0], *tables,
    )
    block, query, key, value, filt, weight = pl.pallas_call(
        finish,
        name="finish",
        out_shape=(
            jax.ShapeDtypeStruct((128, 2048), BF),
            jax.ShapeDtypeStruct((128, 2048), BF),
            jax.ShapeDtypeStruct((128, 2048), BF),
            jax.ShapeDtypeStruct((128, 2048), BF),
            jax.ShapeDtypeStruct((2048, 128), F32),
            jax.ShapeDtypeStruct((128, 2048), F32),
        ),
        in_specs=[anywhere] * 6,
        out_specs=[anywhere] * 6,
        scratch_shapes=[
            vm((2048, 128), BF), vm((128, 2048), BF), vm((2048, 128), F32), vm((128, 2048), F32),
            vm((4, 128, 2048), BF), dma((12,)),
        ],
        compiler_params=pltpu.CompilerParams(vmem_limit_bytes=58 << 20),
    )(block, query, key, value, filt.reshape(2048, 128), weight.reshape(128, 2048))
    return block[None], query[None], key[None], value[None], filt, weight


def solution(mesh):
    rows = P("dp", "ctx", None)
    return jax.shard_map(
        shards,
        mesh=mesh,
        in_specs=(rows, rows, rows, P(None, "ctx"), P("ctx", None), rows),
        out_specs=(rows, rows, rows, rows, P(None, "ctx"), P("ctx", None)),
        check_vma=False,
    )
```
